128 devices in a mesh: leaf: 32 (over y, z, core), sub: 4 (over x).
Axes of the slice: x: 4, y: 4, z: 4, core: 2. Of those that a mesh axis runs over, the one named last changes fastest.
Arguments:
- loads: bfloat16 [16, 1048576], P(None, ('leaf', 'sub')), may hold values from -6 to 6
- col_basis: bfloat16 [8192, 128, 64], P(('leaf', 'sub')), may hold values from -0.5 to 0.5
- row_basis: bfloat16 [8192, 128, 64], P(('leaf', 'sub')), may hold values from -0.75 to 0.75
- near_blocks: bfloat16 [8192, 6, 128, 128], P(('leaf', 'sub')), may hold values from -0.21875 to 0.21875
- near_src: int32 [8192, 6], P(('leaf', 'sub')), may hold values from 0 to 8191, as said below
- up_leaf: bfloat16 [8192, 64, 64], P(('leaf', 'sub')), may hold values from -0.25 to 0.25
- down_leaf: bfloat16 [8192, 64, 64], P(('leaf', 'sub')), may hold values from -0.75 to 0.75
- up_node: bfloat16 [1024, 64, 64], P(('leaf', 'sub')), may hold values from -0.25 to 0.25
- down_node: bfloat16 [1024, 64, 64], P(('leaf', 'sub')), may hold values from -0.75 to 0.75
- up_group: bfloat16 [128, 64, 64], P(('leaf', 'sub')), may hold values from -0.375 to 0.375
- down_group: bfloat16 [128, 64, 64], P(('leaf', 'sub')), may hold values from -0.75 to 0.75
- up_top: bfloat16 [32, 64, 64], replicated, may hold values from -0.375 to 0.375
- downward_top_transfer: bfloat16 [32, 64, 64], replicated, may hold values from -0.75 to 0.75
- coupling: bfloat16 [316, 64, 64], replicated, may hold values from -0.25 to 0.25
- send_table: int32 [128, 21, 48], P(('leaf', 'sub')), may hold values from 0 to 63
- distant_leaf_slot_index: int32 [8192, 8], P(('leaf', 'sub')), may hold values from 0 to 1007, as said below
- far_leaf_type: int32 [8192, 8], P(('leaf', 'sub')), may hold values from 0 to 315
- far_group_src: int32 [32, 8], P('leaf'), may hold values from 0 to 31
- far_group_type: int32 [32, 8], P('leaf'), may hold values from 0 to 315
- far_top_src: int32 [8, 8], replicated, may hold values from 0 to 7
- far_top_type: int32 [8, 8], replicated, may hold values from 0 to 315
Outputs:
- potential: float32 [16, 1048576], P(None, ('leaf', 'sub'))
The draws below stay inside these ranges and needn't reach their ends.
Inputs may be any that keep to these rules, and one draw needn't show every extreme that they name: `near_src`: the first three entries of row t are t, t - 32 and t + 32, clipped to the leaves; every entry lies within 32 of t. `distant_leaf_slot_index`: for a leaf on device e, entry s names a device e + s // 48 - 10 that exists.
All inputs are finite; a program needn't handle non-finite values.
Results may differ from the reference program's by a relative error of at most 0.025.
Values may be sent and summed in bfloat16 or wider, within the bound.
No kernel may reach another device: no remote copies, remote signals or barrier semaphores. Data moves between devices by JAX's collectives and lax.ppermute only.
A program may use at most 128 MiB of HBM per device.

```python
import jax
import jax.numpy as jnp
from jax import lax

NRHS = 16
R = 64
P_SIZE = 128
LEAF_DEV = 64
NEAR = 6
FAR = 8
REACH = 10
SLOTS = 48
TYPES = 316
HALO = 32
LEAVES = 8192
PANELS = 1048576
NODES = 1024
TOP_NODES = 8
N_LEAF = 32
N_SUB = 4
DEVICES = 128


def draw_near_src(key, part):
    key = jax.random.fold_in(key, 3)
    leaf_ids = jnp.arange(LEAVES, dtype=jnp.int32)[:, None]
    offsets = jax.random.randint(key, (LEAVES, NEAR - 3), -HALO, HALO + 1, dtype=jnp.int32)
    fixed = jnp.broadcast_to(jnp.array([0, -HALO, HALO], dtype=jnp.int32), (LEAVES, 3))
    spread = jnp.concatenate([fixed, offsets], axis=1)
    return jnp.clip(leaf_ids + spread, 0, LEAVES - 1).astype(jnp.int32)


def draw_distant_leaf_slot_index(key, part):
    key = jax.random.fold_in(key, 5)
    offset_key, slot_key = jax.random.split(key)
    owner = (jnp.arange(LEAVES, dtype=jnp.int32) // LEAF_DEV)[:, None]
    offsets = jax.random.randint(offset_key, (LEAVES, FAR), -REACH, REACH + 1, dtype=jnp.int32)
    sender = jnp.clip(owner + offsets, 0, DEVICES - 1)
    offset_pos = sender - owner + REACH
    slot_location = jax.random.randint(slot_key, (LEAVES, FAR), 0, SLOTS, dtype=jnp.int32)
    return (offset_pos * SLOTS + slot_location).astype(jnp.int32)


def set_ends(entries, own_key, low, high):
    longest = entries.shape.index(max(entries.shape))
    spots = []
    for shift in (0, 1):
        where = [jax.random.randint(jax.random.fold_in(own_key, axis), (), 0, length) for axis, length in enumerate(entries.shape)]
        where[longest] = (where[longest] + shift) % entries.shape[longest]
        spots.append(tuple(where))
    return entries.at[spots[0]].set(low).at[spots[1]].set(high)


def level_of(stream_key, shape, cuts, low, high):
    def one(dim, blocks):
        steps = jax.random.uniform(jax.random.fold_in(jax.random.fold_in(stream_key, 6), dim), (blocks,), jnp.float32, low / len(cuts), high / len(cuts))
        return jnp.repeat(jnp.exp(steps), shape[dim] // blocks).reshape((-1,) + (1,) * (len(shape) - dim - 1))

    level = one(*cuts[0])
    for cut in cuts[1:]:
        level = level * one(*cut)
    return level


def centred(stream_key, dims, scale, most, shards=(), held_as=jnp.bfloat16):
    values = scale * jax.random.normal(stream_key, dims, jnp.float32)
    if shards:
        values = values * level_of(stream_key, dims, shards, -0.22, 0.18)
    return jnp.clip(values, -most, most).astype(held_as)


def setup_inputs(seed: int = 0) -> dict:
    key_of = jax.random.split(jax.random.key(seed), 22)
    loads = centred(key_of[0], (NRHS, PANELS), 1.0, 6.0, ((1, 128),))
    col_basis = centred(key_of[1], (LEAVES, P_SIZE, R), P_SIZE ** -0.5, 0.5, ((0, 128),))
    row_basis = centred(key_of[2], (LEAVES, P_SIZE, R), R ** -0.5, 0.75, ((0, 128),))
    near_blocks = centred(key_of[3], (LEAVES, NEAR, P_SIZE, P_SIZE), (NEAR * P_SIZE) ** -0.5, 0.21875, ((0, 128),))
    near_src = draw_near_src(jax.random.fold_in(key_of[21], 71), 0)
    up_leaf = centred(key_of[5], (LEAVES, R, R), (8 * R) ** -0.5, 0.25, ((0, 128),))
    down_leaf = centred(key_of[6], (LEAVES, R, R), R ** -0.5, 0.75, ((0, 128),))
    up_node = centred(key_of[7], (NODES, R, R), (LEAF_DEV // 8 * R) ** -0.5, 0.25, ((0, 128),))
    down_node = centred(key_of[8], (NODES, R, R), R ** -0.5, 0.75, ((0, 128),))
    up_group = centred(key_of[9], (DEVICES, R, R), (N_SUB * R) ** -0.5, 0.375, ((0, 128),))
    down_group = centred(key_of[10], (DEVICES, R, R), R ** -0.5, 0.75, ((0, 128),))
    up_top = centred(key_of[11], (N_LEAF, R, R), (4 * R) ** -0.5, 0.375)
    downward_top_transfer = centred(key_of[12], (N_LEAF, R, R), R ** -0.5, 0.75)
    coupling = centred(key_of[13], (TYPES, R, R), (FAR * R) ** -0.5, 0.25)
    send_table = set_ends(jax.random.randint(key_of[14], (DEVICES, 2 * REACH + 1, SLOTS), 0, LEAF_DEV), jax.random.fold_in(key_of[14], 1), 0, LEAF_DEV - 1).astype(jnp.int32)
    distant_leaf_slot_index = draw_distant_leaf_slot_index(jax.random.fold_in(key_of[21], 71), 0)
    far_leaf_type = set_ends(jax.random.randint(key_of[16], (LEAVES, FAR), 0, TYPES), jax.random.fold_in(key_of[16], 1), 0, TYPES - 1).astype(jnp.int32)
    far_group_src = set_ends(jax.random.randint(key_of[17], (N_LEAF, FAR), 0, N_LEAF), jax.random.fold_in(key_of[17], 1), 0, N_LEAF - 1).astype(jnp.int32)
    far_group_type = set_ends(jax.random.randint(key_of[18], (N_LEAF, FAR), 0, TYPES), jax.random.fold_in(key_of[18], 1), 0, TYPES - 1).astype(jnp.int32)
    far_top_src = set_ends(jax.random.randint(key_of[19], (TOP_NODES, FAR), 0, TOP_NODES), jax.random.fold_in(key_of[19], 1), 0, TOP_NODES - 1).astype(jnp.int32)
    far_top_type = set_ends(jax.random.randint(key_of[20], (TOP_NODES, FAR), 0, TYPES), jax.random.fold_in(key_of[20], 1), 0, TYPES - 1).astype(jnp.int32)
    return dict(loads=loads, col_basis=col_basis, row_basis=row_basis, near_blocks=near_blocks, near_src=near_src, up_leaf=up_leaf, down_leaf=down_leaf, up_node=up_node, down_node=down_node, up_group=up_group, down_group=down_group, up_top=up_top, downward_top_transfer=downward_top_transfer, coupling=coupling, send_table=send_table, distant_leaf_slot_index=distant_leaf_slot_index, far_leaf_type=far_leaf_type, far_group_src=far_group_src, far_group_type=far_group_type, far_top_src=far_top_src, far_top_type=far_top_type)


def couple(expansion_weights, source_charges, interaction_kinds, coupling):
    picked = expansion_weights[source_charges].astype(jnp.float32)
    mats = coupling[interaction_kinds].astype(jnp.float32)
    return jnp.einsum("nkvr,nkrs->nvs", picked, mats)


def reference(loads, col_basis, row_basis, near_blocks, near_src, up_leaf, down_leaf, up_node, down_node, up_group, down_group, up_top, downward_top_transfer, coupling, send_table, distant_leaf_slot_index, far_leaf_type, far_group_src, far_group_type, far_top_src, far_top_type):
    leaves = col_basis.shape[0]
    node_count = leaves // 8
    per_dev = LEAF_DEV // 8
    blocks = loads.reshape(NRHS, leaves, P_SIZE)
    leaf_coeff = jnp.einsum("vlp,lpr->lvr", blocks.astype(jnp.float32), col_basis.astype(jnp.float32)).astype(jnp.bfloat16)
    node_coeff = jnp.einsum("ncvr,ncrs->nvs", leaf_coeff.reshape(node_count, 8, NRHS, R).astype(jnp.float32), up_leaf.reshape(node_count, 8, R, R).astype(jnp.float32)).astype(jnp.bfloat16)
    mid_coeff = jnp.einsum("dnvr,dnrs->dvs", node_coeff.reshape(DEVICES, per_dev, NRHS, R).astype(jnp.float32), up_node.reshape(DEVICES, per_dev, R, R).astype(jnp.float32)).astype(jnp.bfloat16)
    group_terms = jnp.einsum("dvr,drs->dvs", mid_coeff.astype(jnp.float32), up_group.astype(jnp.float32))
    group_coeff = group_terms.reshape(N_LEAF, N_SUB, NRHS, R).sum(1).astype(jnp.bfloat16)
    top_coeff = jnp.einsum("gcvr,gcrs->gvs", group_coeff.reshape(TOP_NODES, 4, NRHS, R).astype(jnp.float32), up_top.reshape(TOP_NODES, 4, R, R).astype(jnp.float32)).astype(jnp.bfloat16)
    top_local = couple(top_coeff, far_top_src, far_top_type, coupling).astype(jnp.bfloat16)
    inherited_top = jnp.einsum("gvr,grs->gvs", jnp.repeat(top_local, 4, axis=0).astype(jnp.float32), downward_top_transfer.astype(jnp.float32))
    group_local = (couple(group_coeff, far_group_src, far_group_type, coupling) + inherited_top).astype(jnp.bfloat16)
    mid_local = jnp.einsum("dvr,drs->dvs", jnp.repeat(group_local, N_SUB, axis=0).astype(jnp.float32), down_group.astype(jnp.float32)).astype(jnp.bfloat16)
    node_local = jnp.einsum("dvr,dnrs->dnvs", mid_local.astype(jnp.float32), down_node.reshape(DEVICES, per_dev, R, R).astype(jnp.float32)).astype(jnp.bfloat16)

    def device_part(inputs):
        index, source_charges, interaction_kinds, node_loc, down, near_ids, near_mats, rows = inputs
        offset_pos = (source_charges // SLOTS).astype(jnp.int32)
        slot_location = (source_charges % SLOTS).astype(jnp.int32)
        sender = (index + offset_pos - REACH).astype(jnp.int32)
        leaf_ids = (sender * LEAF_DEV + send_table[sender, offset_pos, slot_location]).astype(jnp.int32)
        far_part = couple(leaf_coeff, leaf_ids, interaction_kinds, coupling)
        inherited = jnp.einsum("nvr,ncrs->ncvs", node_loc.astype(jnp.float32), down.reshape(per_dev, 8, R, R).astype(jnp.float32)).reshape(LEAF_DEV, NRHS, R)
        leaf_local = (far_part + inherited).astype(jnp.bfloat16)
        far_field = jnp.einsum("lvr,lpr->vlp", leaf_local.astype(jnp.float32), rows.astype(jnp.float32))
        gathered = blocks[:, near_ids].astype(jnp.float32)
        near_field = jnp.einsum("vlkq,lkpq->vlp", gathered, near_mats.astype(jnp.float32))
        return far_field + near_field

    product_outputs = lax.map(device_part, (
        jnp.arange(DEVICES, dtype=jnp.int32),
        distant_leaf_slot_index.reshape(DEVICES, LEAF_DEV, FAR),
        far_leaf_type.reshape(DEVICES, LEAF_DEV, FAR),
        node_local,
        down_leaf.reshape(DEVICES, LEAF_DEV, R, R),
        near_src.reshape(DEVICES, LEAF_DEV, NEAR),
        near_blocks.reshape(DEVICES, LEAF_DEV, NEAR, P_SIZE, P_SIZE),
        row_basis.reshape(DEVICES, LEAF_DEV, P_SIZE, R)))
    return jnp.transpose(product_outputs, (1, 0, 2, 3)).reshape(NRHS, leaves * P_SIZE)
```

```python
import functools

import jax
import jax.numpy as jnp
from jax import lax
from jax.experimental import pallas as pl
from jax.experimental.pallas import tpu as pltpu
from jax.sharding import PartitionSpec as P

AXES = ("leaf", "sub")
DEVICES = 128
RANK = 64
PANEL = 128
LEAVES = 64
FAR = 8
NEAR = 6
HALO = 32
OFFSETS = 21
SLOTS = 48
TYPES = 316
TYPE_ROWS = 320
TERM_ROW = 512
TABLE_ROW = 528
BLOCK = 560
KP_ROWS = 576
NT = (((1,), (1,)), ((), ()))


def dot(a, b):
    return jnp.dot(a, b, preferred_element_type=jnp.float32)


def dot_nt(a, b):
    return lax.dot_general(a, b, NT, preferred_element_type=jnp.float32)


def lane_index(rows):
    return lax.broadcasted_iota(jnp.int32, (rows, 128), 1)


def moved(value, pairs):
    return lax.ppermute(value, AXES, pairs)


def line_shift(steps):
    return [(s, s + steps) for s in range(max(0, -steps), min(DEVICES, DEVICES - steps))]


def x_shift(d):
    return [(p, (p & ~3) | ((p + d) & 3)) for p in range(DEVICES)]


def z_shift(d):
    return [(p, (p & ~24) | ((p + 8 * d) & 24)) for p in range(DEVICES)]


def y_shift(d):
    return [(p, (p + 32 * d) % DEVICES) for p in range(DEVICES)]


CORE_SWAP = [(p, p ^ 4) for p in range(DEVICES)]


def two_blocks_away(near_edge, steps):
    pairs = []
    for e in range(DEVICES):
        i = e % 8
        if i < near_edge and e >= steps:
            pairs.append((e - steps, e))
        if i >= 8 - near_edge and e + steps < DEVICES:
            pairs.append((e + steps, e))
    return pairs


def up_kernel(x_ref, cb_ref, ul_ref, un_ref, ug_ref, table_ref, out_ref, mid_ref):
    step = pl.program_id(0)
    nodes = ul_ref.shape[0]
    left = lane_index(16) < RANK

    @pl.when(step == 0)
    def _():
        mid_ref[...] = jnp.zeros_like(mid_ref)

    mid = mid_ref[...]
    for n in range(nodes):
        blocks = []
        for q in range(4):
            i = n * 4 + q
            lhs = jnp.concatenate(
                [x_ref[:, 2 * i * PANEL : (2 * i + 1) * PANEL], x_ref[:, (2 * i + 1) * PANEL : (2 * i + 2) * PANEL]],
                axis=0,
            )
            both = dot_nt(lhs, cb_ref[i])
            block = jnp.where(left, both[:16], both[16:]).astype(jnp.bfloat16)
            row = pl.multiple_of(step * (nodes * 64) + i * 16, 16)
            out_ref[pl.ds(row, 16), :] = block
            blocks.append(block)
        node = dot(jnp.concatenate(blocks, axis=1), ul_ref[n]).astype(jnp.bfloat16)
        mid = mid + dot(node, un_ref[n])
    mid_ref[...] = mid

    @pl.when(step == pl.num_programs(0) - 1)
    def _():
        term = dot(mid.astype(jnp.bfloat16), ug_ref[...])
        high = term.astype(jnp.bfloat16).astype(jnp.float32)
        parts = jnp.concatenate([high, term - high], axis=1)
        out_ref[TERM_ROW : TERM_ROW + 16, :] = parts.astype(jnp.bfloat16)
        out_ref[TABLE_ROW:BLOCK, :] = table_ref[...].astype(jnp.bfloat16)


def up_sweep(loads, col_basis, up_leaf, up_node, up_group, table):
    steps = 4
    return pl.pallas_call(
        up_kernel,
        grid=(steps,),
        in_specs=[
            pl.BlockSpec((16, 8192 // steps), lambda i: (0, i)),
            pl.BlockSpec((32 // steps, 128, 128), lambda i: (i, 0, 0)),
            pl.BlockSpec((8 // steps, 512, RANK), lambda i: (i, 0, 0)),
            pl.BlockSpec((8 // steps, RANK, RANK), lambda i: (i, 0, 0)),
            pl.BlockSpec((RANK, RANK), lambda i: (0, 0)),
            pl.BlockSpec((32, 128), lambda i: (0, 0)),
        ],
        out_specs=pl.BlockSpec((BLOCK, 128), lambda i: (0, 0)),
        out_shape=jax.ShapeDtypeStruct((BLOCK, 128), jnp.bfloat16),
        scratch_shapes=[pltpu.VMEM((16, RANK), jnp.float32)],
        compiler_params=pltpu.CompilerParams(vmem_limit_bytes=32 << 20),
        cost_estimate=pl.CostEstimate(flops=40_000_000, bytes_accessed=2_600_000, transcendentals=0),
        name="up_sweep",
    )(loads, col_basis, up_leaf, up_node, up_group, table)


def pick_kernel(place, leaf_type, group_type, top_type, k2_ref, down_ref, out_ref, table):
    step = pl.program_id(0)
    per_step = k2_ref.shape[0] // RANK
    eye = (
        lax.broadcasted_iota(jnp.int32, (TYPE_ROWS, TYPES), 0)
        == lax.broadcasted_iota(jnp.int32, (TYPE_ROWS, TYPES), 1)
    ).astype(jnp.bfloat16)
    for r in range(0, per_step, 2):
        one = k2_ref[r * RANK : (r + 1) * RANK, :]
        two = k2_ref[(r + 1) * RANK : (r + 2) * RANK, :]
        turned = dot_nt(eye, jnp.concatenate([one, one, two, two], axis=0))
        row = pl.multiple_of((step * per_step + r) * TYPE_ROWS, 8)
        table[pl.ds(row, TYPE_ROWS), :] = turned[:, :128]
        table[pl.ds(row + TYPE_ROWS, TYPE_ROWS), :] = turned[:, 128:]

    @pl.when(step == pl.num_programs(0) - 1)
    def _():
        left = lane_index(RANK) < RANK

        def pair(i, first, second):
            one = table[pl.ds(first, RANK, stride=TYPE_ROWS), :]
            two = table[pl.ds(second, RANK, stride=TYPE_ROWS), :]
            return jnp.where(left, one, two).astype(jnp.bfloat16)

        @pl.loop(0, LEAVES // 2)
        def _(i):
            base = pl.multiple_of(i * KP_ROWS, 64)
            for k in range(FAR):
                out_ref[pl.ds(base + k * RANK, RANK), :] = pair(i, leaf_type[k, 2 * i], leaf_type[k, 2 * i + 1])
            out_ref[pl.ds(base + FAR * RANK, RANK), :] = jnp.concatenate(
                [down_ref[2 * i], down_ref[2 * i + 1]], axis=1
            )

        base = LEAVES // 2 * KP_ROWS
        parent = place[5]
        for k in range(FAR):
            out_ref[base + k * RANK : base + (k + 1) * RANK, :] = pair(0, group_type[0, k], top_type[parent, k])
        out_ref[base + FAR * RANK : base + KP_ROWS, :] = jnp.zeros((RANK, 128), jnp.bfloat16)


def picked_couplings(place, leaf_type, group_type, top_type, coupling, down_leaf):
    steps = 8
    rows = (LEAVES // 2 + 1) * KP_ROWS
    smem = pl.BlockSpec(memory_space=pltpu.SMEM)
    return pl.pallas_call(
        pick_kernel,
        grid=(steps,),
        in_specs=[
            smem,
            smem,
            smem,
            smem,
            pl.BlockSpec((RANK * RANK // steps, TYPES), lambda i: (i, 0)),
            pl.BlockSpec((LEAVES, RANK, RANK), lambda i: (0, 0, 0)),
        ],
        out_specs=pl.BlockSpec((rows, 128), lambda i: (0, 0)),
        out_shape=jax.ShapeDtypeStruct((rows, 128), jnp.bfloat16),
        scratch_shapes=[pltpu.VMEM((RANK * TYPE_ROWS, 128), jnp.float32)],
        compiler_params=pltpu.CompilerParams(vmem_limit_bytes=48 << 20),
        cost_estimate=pl.CostEstimate(flops=3_200_000_000, bytes_accessed=9_000_000, transcendentals=0),
        name="pick_couplings",
    )(place, leaf_type, group_type, top_type, coupling, down_leaf)


def near_kernel(first, per_step, place, src, low_ref, own_ref, high_ref, blocks_ref, out_ref, all_x):
    step = pl.program_id(0)

    @pl.when(step == 0)
    def _():
        all_x[:, : HALO * PANEL] = low_ref[...]
        all_x[:, HALO * PANEL : (HALO + LEAVES) * PANEL] = own_ref[...]
        all_x[:, (HALO + LEAVES) * PANEL :] = high_ref[...]

    start = place[0] * LEAVES - HALO
    for t in range(per_step):
        total = jnp.zeros((16, PANEL), jnp.float32)
        for k in range(NEAR):
            i = src[k, first + step * per_step + t] - start
            x = all_x[:, pl.ds(pl.multiple_of(i * PANEL, PANEL), PANEL)]
            total = total + dot_nt(x, blocks_ref[t, k])
        out_ref[:, t * PANEL : (t + 1) * PANEL] = total


def near_field(place, src, low, own, high, blocks, first, count):
    per_step = 8
    smem = pl.BlockSpec(memory_space=pltpu.SMEM)
    begin = first // per_step
    return pl.pallas_call(
        functools.partial(near_kernel, first, per_step),
        grid=(count // per_step,),
        in_specs=[
            smem,
            smem,
            pl.BlockSpec(low.shape, lambda i: (0, 0)),
            pl.BlockSpec(own.shape, lambda i: (0, 0)),
            pl.BlockSpec(high.shape, lambda i: (0, 0)),
            pl.BlockSpec((per_step, NEAR, PANEL, PANEL), lambda i: (begin + i, 0, 0, 0)),
        ],
        out_specs=pl.BlockSpec((16, per_step * PANEL), lambda i: (0, i)),
        out_shape=jax.ShapeDtypeStruct((16, count * PANEL), jnp.float32),
        scratch_shapes=[pltpu.VMEM((16, (2 * HALO + LEAVES) * PANEL), jnp.bfloat16)],
        compiler_params=pltpu.CompilerParams(vmem_limit_bytes=32 << 20),
        cost_estimate=pl.CostEstimate(flops=count * 3_200_000, bytes_accessed=count * 200_000, transcendentals=0),
        name="near_field",
    )(place, src, low, own, high, blocks)


def group_sum_kernel(own_ref, other_ref, place, out_ref):
    def total(ref):
        parts = [ref[d, TERM_ROW : TERM_ROW + 16, :].astype(jnp.float32) for d in range(4)]
        both = (parts[0] + parts[1]) + (parts[2] + parts[3])
        return (both + pltpu.roll(both, RANK, 1)).astype(jnp.bfloat16)

    own, other = total(own_ref), total(other_ref)
    left = lane_index(16) < RANK
    first_core = jnp.full((16, 128), place[3], jnp.int32) == 0
    out_ref[...] = jnp.where(left == first_core, own, other)


def group_sums(own, other, place):
    return pl.pallas_call(
        group_sum_kernel,
        in_specs=[
            pl.BlockSpec(own.shape, lambda: (0, 0, 0)),
            pl.BlockSpec(other.shape, lambda: (0, 0, 0)),
            pl.BlockSpec(memory_space=pltpu.SMEM),
        ],
        out_shape=jax.ShapeDtypeStruct((16, 128), jnp.bfloat16),
        name="group_sums",
    )(own, other, place)


def down_kernel(place, far_src, top_src, groups_ref, ut_ref, dt_ref, kp_ref, dg_ref, dn_ref, out_ref, tops):
    y, z, parent, group = place[1], place[2], place[5], place[6]
    left = lane_index(16) < RANK

    def block(yy, zz):
        at = ((z - zz) & 3) * 4 + ((y - yy) & 3)
        return groups_ref[pl.ds(pl.multiple_of(at * 16, 16), 16), :]

    for h in range(8):
        yy, zz = h // 2, 2 * (h % 2)
        four = jnp.concatenate([block(yy, zz), block(yy, zz + 1)], axis=1)
        tops[h] = dot(four, ut_ref[h]).astype(jnp.bfloat16)
    by_group = jnp.zeros((16, 128), jnp.float32)
    by_top = jnp.zeros((16, 128), jnp.float32)
    for k in range(FAR):
        g = far_src[0, k]
        pair = block(g >> 3, (g >> 1) & 3).astype(jnp.float32)
        pair = jnp.where(jnp.full((16, 128), g & 1, jnp.int32) == 1, pltpu.roll(pair, RANK, 1), pair)
        both = kp_ref[k * RANK : (k + 1) * RANK, :]
        by_group = by_group + dot(pair[:, :RANK].astype(jnp.bfloat16), both)
        by_top = by_top + dot(tops[top_src[parent, k]], both)
    top_local = by_top[:, RANK:].astype(jnp.bfloat16)
    group_local = (by_group[:, :RANK] + dot(top_local, dt_ref[group])).astype(jnp.bfloat16)
    mid_local = dot(group_local, dg_ref[...]).astype(jnp.bfloat16)
    for n in range(8):
        out_ref[n * 16 : (n + 1) * 16, :] = dot(mid_local, dn_ref[n]).astype(jnp.bfloat16)


def down_sweep(place, far_src, top_src, groups, up_top, down_top, picked, down_group, down_node):
    smem = pl.BlockSpec(memory_space=pltpu.SMEM)
    last = LEAVES // 2
    return pl.pallas_call(
        down_kernel,
        grid=(1,),
        in_specs=[
            smem,
            smem,
            smem,
            pl.BlockSpec((256, 128), lambda i: (0, 0)),
            pl.BlockSpec((8, 256, RANK), lambda i: (0, 0, 0)),
            pl.BlockSpec((32, RANK, RANK), lambda i: (0, 0, 0)),
            pl.BlockSpec((KP_ROWS, 128), lambda i: (last, 0)),
            pl.BlockSpec((RANK, RANK), lambda i: (0, 0)),
            pl.BlockSpec((8, RANK, RANK), lambda i: (0, 0, 0)),
        ],
        out_specs=pl.BlockSpec((128, RANK), lambda i: (0, 0)),
        out_shape=jax.ShapeDtypeStruct((128, RANK), jnp.bfloat16),
        scratch_shapes=[pltpu.VMEM((8, 16, RANK), jnp.bfloat16)],
        compiler_params=pltpu.CompilerParams(vmem_limit_bytes=32 << 20),
        cost_estimate=pl.CostEstimate(flops=20_000_000, bytes_accessed=1_500_000, transcendentals=0),
        name="down_sweep",
    )(place, far_src, top_src, groups, up_top, down_top, picked, down_group, down_node)


def far_kernel(
    place, slot_ref, g0, g1, z0, z1, z2, z3, e0, e1, picked, rows_ref, node_ref, near0, near1, out_ref,
    table, kp, found, scalars, sems, kp_sems, scalar_sem,
):
    copies = []
    for j, ref in enumerate((g0, g1, z0, z1, z2, z3)):
        copies.append(pltpu.make_async_copy(ref, table.at[pl.ds(j * 4 * BLOCK, 4 * BLOCK), :], sems.at[j]))
    for j, ref in enumerate((e0, e1)):
        copies.append(pltpu.make_async_copy(ref, table.at[pl.ds((24 + j) * BLOCK, BLOCK), :], sems.at[6 + j]))
    for c in copies:
        c.start()
    chunks = kp_sems.shape[0]
    size = LEAVES // 2 * KP_ROWS // chunks
    kp_copies = [
        pltpu.make_async_copy(
            picked.at[pl.ds(j * size, size), :], kp.at[pl.ds(j * size, size), :], kp_sems.at[j]
        )
        for j in range(chunks)
    ]
    for c in kp_copies:
        c.start()

    x, core = place[4], place[3]
    i_in_block = core * 4 + x

    def slot_of(offset):
        at = i_in_block + offset
        away = at >> 3
        d = (x - at) & 3
        same = jnp.where(((at >> 2) & 1) == core, 0, 4)
        base = jnp.where(away == 0, 0, jnp.where(away < 0, 8, 16))
        inside = base + same + d
        far = jnp.where((offset == 10) | (offset == -10), 24, 25)
        return jnp.where((away > 1) | (away < -1), far, inside)

    slots = slot_ref[...]
    j_of = (slots * 1366) >> 16
    c_of = slots - j_of * SLOTS
    row_of = slot_of(j_of - 10) * BLOCK
    for c in copies:
        c.wait()
    leaf = jnp.zeros_like(slots)
    for j in range(OFFSETS):
        row = slot_of(jnp.int32(j - 10)) * BLOCK + TABLE_ROW + (j // 16) * 16
        rows = table[pl.ds(pl.multiple_of(row, 16), 16), :].astype(jnp.float32)
        line = jnp.broadcast_to(rows[j % 16 : j % 16 + 1, :], (8, 128)).astype(jnp.int32)
        here = jnp.take_along_axis(line, c_of, axis=1)
        leaf = jnp.where(j_of == j, here, leaf)
    leaf = leaf & (LEAVES - 1)
    found[...] = (row_of + (leaf >> 1) * 16) * 2 + (leaf & 1)
    to_scalars = pltpu.make_async_copy(found, scalars, scalar_sem)
    to_scalars.start()
    to_scalars.wait()

    left = lane_index(16) < RANK
    left_pair = lane_index(32) < RANK
    top_half = lax.broadcasted_iota(jnp.int32, (32, 128), 0) < 16

    def source(k, t, want):
        code = scalars[k, t]
        block = table[pl.ds(pl.multiple_of((code >> 1), 16), 16), :].astype(jnp.float32)
        return pltpu.roll(block, ((code & 1) ^ want) * RANK, 1)

    def coefficients(t):
        parts = []
        for m in range(FAR // 2):
            parts.append(jnp.where(left, source(2 * m, t, 0), source(2 * m + 1, t, 1)).astype(jnp.bfloat16))
        return jnp.concatenate(parts, axis=1)

    pairs = LEAVES // 2 // chunks
    for j in range(chunks):
        kp_copies[j].wait()

        @pl.loop(0, pairs)
        def _(q):
            i = j * pairs + q
            two = jnp.concatenate([coefficients(2 * i), coefficients(2 * i + 1)], axis=0)
            node = node_ref[pl.ds(pl.multiple_of((i // 4) * 16, 16), 16), :]
            node = jnp.concatenate([node, node], axis=0)
            base = pl.multiple_of(i * KP_ROWS, 64)
            local = dot(two, kp[pl.ds(base, FAR * RANK), :]) + dot(node, kp[pl.ds(base + FAR * RANK, RANK), :])
            local = jnp.where(left_pair == top_half, local, 0.0).astype(jnp.bfloat16)
            both = dot(local, rows_ref[i])
            near_ref = near0 if j < chunks // 2 else near1
            shift = 0 if j < chunks // 2 else LEAVES // 2 * PANEL
            at = pl.multiple_of(i * (2 * PANEL), 2 * PANEL)
            near_at = pl.multiple_of(i * (2 * PANEL) - shift, 2 * PANEL)
            near = near_ref[:, pl.ds(near_at, 2 * PANEL)]
            out_ref[:, pl.ds(at, 2 * PANEL)] = jnp.concatenate([both[:16], both[16:]], axis=1) + near


def far_field(place, slots, pieces, extras, picked, row_basis, node_local, near):
    smem = pl.BlockSpec(memory_space=pltpu.SMEM)
    hbm = pl.BlockSpec(memory_space=pl.ANY)
    chunks = 4
    return pl.pallas_call(
        far_kernel,
        grid=(1,),
        in_specs=[smem, pl.BlockSpec((8, 128), lambda i: (0, 0))]
        + [hbm] * 9
        + [
            pl.BlockSpec((LEAVES // 2, 128, 128), lambda i: (0, 0, 0)),
            pl.BlockSpec((128, RANK), lambda i: (0, 0)),
            pl.BlockSpec((16, LEAVES // 2 * PANEL), lambda i: (0, 0)),
            pl.BlockSpec((16, LEAVES // 2 * PANEL), lambda i: (0, 0)),
        ],
        out_specs=pl.BlockSpec((16, LEAVES * PANEL), lambda i: (0, 0)),
        out_shape=jax.ShapeDtypeStruct((16, LEAVES * PANEL), jnp.float32),
        scratch_shapes=[
            pltpu.VMEM((26 * BLOCK, 128), jnp.bfloat16),
            pltpu.VMEM((LEAVES // 2 * KP_ROWS, 128), jnp.bfloat16),
            pltpu.VMEM((8, 128), jnp.int32),
            pltpu.SMEM((8, 128), jnp.int32),
            pltpu.SemaphoreType.DMA((8,)),
            pltpu.SemaphoreType.DMA((chunks,)),
            pltpu.SemaphoreType.DMA,
        ],
        compiler_params=pltpu.CompilerParams(vmem_limit_bytes=48 << 20),
        cost_estimate=pl.CostEstimate(flops=300_000_000, bytes_accessed=11_000_000, transcendentals=0),
        name="far_field",
    )(place, slots, *pieces, *extras, picked, row_basis, node_local, *near)


def per_device(
    loads,
    col_basis,
    row_basis,
    near_blocks,
    near_src,
    up_leaf,
    down_leaf,
    up_node,
    down_node,
    up_group,
    down_group,
    up_top,
    downward_top_transfer,
    coupling,
    send_table,
    distant_leaf_slot_index,
    far_leaf_type,
    far_group_src,
    far_group_type,
    far_top_src,
    far_top_type,
):
    group = lax.axis_index("leaf")
    sub = lax.axis_index("sub")
    pos = group * 4 + sub
    place = jnp.stack([pos, group >> 3, (group >> 1) & 3, group & 1, sub, group >> 2, group, group]).astype(jnp.int32)
    table = jnp.pad(send_table[0], ((0, 32 - OFFSETS), (0, 128 - SLOTS)))
    slots = jnp.pad(distant_leaf_slot_index.T, ((0, 0), (0, 128 - LEAVES)))

    half = HALO * PANEL
    low = moved(loads[:, half:], line_shift(1))
    high = moved(loads[:, :half], line_shift(-1))

    own = up_sweep(
        loads,
        jnp.swapaxes(col_basis, 1, 2).reshape(LEAVES // 2, 128, PANEL),
        up_leaf.reshape(8, 8 * RANK, RANK),
        up_node,
        up_group[0],
        table,
    )
    extra = [moved(own, two_blocks_away(2, 10)), moved(own, two_blocks_away(1, 9))]
    along_x = [moved(own, x_shift(d)) for d in (1, 2, 3)]
    mine = jnp.concatenate([own] + along_x, axis=0)
    theirs = moved(mine, CORE_SWAP)
    below = moved(mine, line_shift(8))
    above = moved(mine, line_shift(-8))

    picked = picked_couplings(
        place,
        far_leaf_type.T,
        far_group_type,
        far_top_type,
        jnp.transpose(coupling, (1, 2, 0)).reshape(RANK * RANK, TYPES),
        down_leaf,
    )
    near = [near_field(place, near_src.T, low, loads, high, near_blocks, f, LEAVES // 2) for f in (0, LEAVES // 2)]

    pair = group_sums(mine.reshape(4, BLOCK, 128), theirs.reshape(4, BLOCK, 128), place)
    column = jnp.concatenate([pair] + [moved(pair, y_shift(d)) for d in (1, 2, 3)], axis=0)
    groups = jnp.concatenate([column] + [moved(column, z_shift(d)) for d in (1, 2, 3)], axis=0)
    node_local = down_sweep(
        place,
        far_group_src,
        far_top_src,
        groups,
        up_top.reshape(8, 4 * RANK, RANK),
        downward_top_transfer,
        picked,
        down_group[0],
        down_node,
    )
    pieces = [mine, theirs, below, moved(below, CORE_SWAP), above, moved(above, CORE_SWAP)]
    return far_field(
        place,
        slots,
        pieces,
        extra,
        picked,
        jnp.swapaxes(row_basis, 1, 2).reshape(LEAVES // 2, 2 * RANK, PANEL),
        node_local,
        near,
    )


def solution(mesh):
    whole, split = P(), P(AXES)
    return jax.shard_map(
        per_device,
        mesh=mesh,
        in_specs=(
            P(None, AXES),
            split, split, split, split, split, split, split, split, split, split,
            whole, whole, whole,
            split, split, split,
            P("leaf"), P("leaf"),
            whole, whole,
        ),
        out_specs=P(None, AXES),
        check_vma=False,
    )
```

```python
import functools

import jax
import jax.numpy as jnp
from jax import lax
from jax.experimental import pallas as pl
from jax.experimental.pallas import tpu as pltpu
from jax.sharding import PartitionSpec as P

AXES = ("leaf", "sub")
DEVICES = 128
RANK = 64
PANEL = 128
LEAVES = 64
FAR = 8
NEAR = 6
HALO = 32
OFFSETS = 21
SLOTS = 48
TYPES = 316
HALF = 32
TYPE_ROWS = 328
VMEM = 60 << 20
TERM_ROW = 512
TABLE_ROW = 528
BLOCK = 560
NT = (((1,), (1,)), ((), ()))


def dot(a, b):
    return jnp.dot(a, b, preferred_element_type=jnp.float32)


def dot_nt(a, b):
    return lax.dot_general(a, b, NT, preferred_element_type=jnp.float32)


def lane_index(rows):
    return lax.broadcasted_iota(jnp.int32, (rows, 128), 1)


def place():
    group, sub = lax.axis_index("leaf"), lax.axis_index("sub")
    return group, sub


def moved(value, pairs):
    return lax.ppermute(value, AXES, pairs)


def line_shift(steps):
    return [(s, s + steps) for s in range(max(0, -steps), min(DEVICES, DEVICES - steps))]


def x_shift(d):
    return [(p, (p & ~3) | ((p + d) & 3)) for p in range(DEVICES)]


def z_shift(d):
    return [(p, (p & ~24) | ((p + 8 * d) & 24)) for p in range(DEVICES)]


def y_shift(d):
    return [(p, (p + 32 * d) % DEVICES) for p in range(DEVICES)]


CORE_SWAP = [(p, p ^ 4) for p in range(DEVICES)]


def two_blocks_away(near_edge, steps):
    pairs = []
    for e in range(DEVICES):
        i = e % 8
        if i < near_edge and e >= steps:
            pairs.append((e - steps, e))
        if i >= 8 - near_edge and e + steps < DEVICES:
            pairs.append((e + steps, e))
    return pairs


def up_kernel(x_ref, cb_ref, ul_ref, un_ref, ug_ref, table_ref, out_ref, mid_ref, lines):
    step = pl.program_id(0)
    nodes = un_ref.shape[0]
    quarter = lane_index(16) // HALF

    @pl.when(step == 0)
    def _():
        mid_ref[...] = jnp.zeros_like(mid_ref)

    mid = mid_ref[...]
    for n in range(nodes):
        node = jnp.zeros((16, RANK), jnp.float32)
        for b in range(2):
            four = range(n * 8 + b * 4, n * 8 + b * 4 + 4)
            x = jnp.concatenate([x_ref[:, t * PANEL : (t + 1) * PANEL] for t in four], axis=0)
            halves = []
            for q in range(2):
                rows = slice(q * HALF, (q + 1) * HALF)
                got = dot_nt(x, jnp.concatenate([cb_ref[t, rows, :] for t in four], axis=0))
                block = got[:16]
                for a in range(1, 4):
                    block = jnp.where(quarter == a, got[a * 16 : (a + 1) * 16], block)
                block = block.astype(jnp.bfloat16)
                halves.append(block)
                node = node + dot(block, jnp.concatenate([ul_ref[t, rows, :] for t in four], axis=0))
            row = pl.multiple_of(step * (nodes * 64) + (n * 2 + b) * 32, 32)
            out_ref[pl.ds(row, 32), :] = jnp.concatenate(halves, axis=0)
        mid = mid + dot(node.astype(jnp.bfloat16), un_ref[n])
    mid_ref[...] = mid

    @pl.when(step == pl.num_programs(0) - 1)
    def _():
        term = dot(mid.astype(jnp.bfloat16), ug_ref[...])
        high = term.astype(jnp.bfloat16).astype(jnp.float32)
        parts = jnp.concatenate([high, term - high], axis=1)
        out_ref[TERM_ROW : TERM_ROW + 16, :] = parts.astype(jnp.bfloat16)
        lines[...] = jnp.zeros_like(lines)
        for j in range(OFFSETS):
            lines[j : j + 1, :SLOTS] = table_ref[j].astype(jnp.float32)
        out_ref[TABLE_ROW:BLOCK, :] = lines[...].astype(jnp.bfloat16)


def up_sweep(loads, col_basis, up_leaf, up_node, up_group, table):
    steps = 2
    return pl.pallas_call(
        up_kernel,
        grid=(steps,),
        in_specs=[
            pl.BlockSpec((16, 8192 // steps), lambda i: (0, i)),
            pl.BlockSpec((LEAVES // steps, RANK, PANEL), lambda i: (i, 0, 0)),
            pl.BlockSpec((LEAVES // steps, RANK, RANK), lambda i: (i, 0, 0)),
            pl.BlockSpec((8 // steps, RANK, RANK), lambda i: (i, 0, 0)),
            pl.BlockSpec((RANK, RANK), lambda i: (0, 0)),
            pl.BlockSpec((OFFSETS, 1, SLOTS), lambda i: (0, 0, 0)),
        ],
        out_specs=pl.BlockSpec((BLOCK, 128), lambda i: (0, 0)),
        out_shape=jax.ShapeDtypeStruct((BLOCK, 128), jnp.bfloat16),
        scratch_shapes=[pltpu.VMEM((16, RANK), jnp.float32), pltpu.VMEM((32, 128), jnp.float32)],
        compiler_params=pltpu.CompilerParams(vmem_limit_bytes=VMEM),
        cost_estimate=pl.CostEstimate(flops=40_000_000, bytes_accessed=2_600_000, transcendentals=0),
        name="up_sweep",
    )(loads, col_basis, up_leaf, up_node, up_group, table)


def turn_kernel(k_ref, out_ref, table):
    step = pl.program_id(0)
    per_step = k_ref.shape[1] // RANK
    for r in range(per_step):
        rows = slice(r * RANK, (r + 1) * RANK)
        both = jnp.concatenate([k_ref[0, rows, :], k_ref[1, rows, :]], axis=0).astype(jnp.float32)
        row = pl.multiple_of((step * per_step + r) * TYPE_ROWS, 8)
        table[pl.ds(row, TYPES), :] = both.T

    @pl.when(step == pl.num_programs(0) - 1)
    def _():
        @pl.loop(0, TYPES // 4)
        def _(i):
            for u in range(4):
                t = i * 4 + u
                matrix = table[pl.ds(t, HALF, stride=TYPE_ROWS), :].astype(jnp.bfloat16)
                out_ref[pl.ds(pl.multiple_of(t * HALF, HALF), HALF), :] = matrix


def turned_couplings(coupling):
    steps = 4
    rows = TYPES * HALF
    return pl.pallas_call(
        turn_kernel,
        grid=(steps,),
        in_specs=[pl.BlockSpec((2, HALF * RANK // steps, TYPES), lambda i: (0, i, 0))],
        out_specs=pl.BlockSpec((rows, 128), lambda i: (0, 0)),
        out_shape=jax.ShapeDtypeStruct((rows, 128), jnp.bfloat16),
        scratch_shapes=[pltpu.VMEM((HALF * TYPE_ROWS, 128), jnp.float32)],
        compiler_params=pltpu.CompilerParams(vmem_limit_bytes=VMEM),
        cost_estimate=pl.CostEstimate(flops=0, bytes_accessed=20_000_000, transcendentals=0),
        name="turn_couplings",
    )(coupling)


def near_kernel(first, per_step, src, low_ref, own_ref, high_ref, blocks_ref, out_ref, all_x):
    step = pl.program_id(0)

    @pl.when(step == 0)
    def _():
        all_x[:, : HALO * PANEL] = low_ref[...]
        all_x[:, HALO * PANEL : (HALO + LEAVES) * PANEL] = own_ref[...]
        all_x[:, (HALO + LEAVES) * PANEL :] = high_ref[...]

    group, sub = place()
    start = (group * 4 + sub) * LEAVES - HALO
    for t in range(per_step):
        x = []
        for k in range(NEAR):
            i = src[k, first + step * per_step + t] - start
            x.append(all_x[:, pl.ds(pl.multiple_of(i * PANEL, PANEL), PANEL)])
        blocks = jnp.concatenate([blocks_ref[t, k] for k in range(NEAR)], axis=1)
        out_ref[:, t * PANEL : (t + 1) * PANEL] = dot_nt(jnp.concatenate(x, axis=1), blocks)


def near_field(src, low, own, high, blocks, first, count):
    per_step = 16
    smem = pl.BlockSpec(memory_space=pltpu.SMEM)
    begin = first // per_step
    return pl.pallas_call(
        functools.partial(near_kernel, first, per_step),
        grid=(count // per_step,),
        in_specs=[
            smem,
            pl.BlockSpec(low.shape, lambda i: (0, 0)),
            pl.BlockSpec(own.shape, lambda i: (0, 0)),
            pl.BlockSpec(high.shape, lambda i: (0, 0)),
            pl.BlockSpec((per_step, NEAR, PANEL, PANEL), lambda i: (begin + i, 0, 0, 0)),
        ],
        out_specs=pl.BlockSpec((16, per_step * PANEL), lambda i: (0, i)),
        out_shape=jax.ShapeDtypeStruct((16, count * PANEL), jnp.float32),
        scratch_shapes=[pltpu.VMEM((16, (2 * HALO + LEAVES) * PANEL), jnp.bfloat16)],
        compiler_params=pltpu.CompilerParams(vmem_limit_bytes=VMEM),
        cost_estimate=pl.CostEstimate(flops=count * 3_200_000, bytes_accessed=count * 300_000, transcendentals=0),
        name="near_field",
    )(src, low, own, high, blocks)


def group_sum_kernel(own_ref, other_ref, out_ref):
    def total(ref):
        parts = [ref[d].astype(jnp.float32) for d in range(4)]
        both = (parts[0] + parts[1]) + (parts[2] + parts[3])
        return (both + pltpu.roll(both, RANK, 1)).astype(jnp.bfloat16)

    own, other = total(own_ref), total(other_ref)
    left = lane_index(16) < RANK
    first_core = jnp.full((16, 128), place()[0] & 1, jnp.int32) == 0
    out_ref[...] = jnp.where(left == first_core, own, other)


def group_sums(own, other):
    terms = pl.BlockSpec((4, 16, 128), lambda i: (0, TERM_ROW // 16, 0))
    return pl.pallas_call(
        group_sum_kernel,
        grid=(1,),
        in_specs=[terms, terms],
        out_specs=pl.BlockSpec((16, 128), lambda i: (0, 0)),
        out_shape=jax.ShapeDtypeStruct((16, 128), jnp.bfloat16),
        compiler_params=pltpu.CompilerParams(vmem_limit_bytes=VMEM),
        name="group_sums",
    )(own, other)


def down_kernel(
    far_src, far_type, top_src, top_type, c0, c1, c2, c3, ut_ref, dt_ref, turned_ref, dg_ref, dn_ref, out_ref,
    groups, tops,
):
    group, _ = place()
    y, z, parent = group >> 3, (group >> 1) & 3, group >> 2
    for j, ref in enumerate((c0, c1, c2, c3)):
        groups[j * 64 : (j + 1) * 64, :] = ref[...]

    def block(yy, zz):
        at = ((z - zz) & 3) * 4 + ((y - yy) & 3)
        return groups[pl.ds(pl.multiple_of(at * 16, 16), 16), :]

    def coupling(kind):
        return turned_ref[pl.ds(pl.multiple_of(kind * HALF, HALF), HALF), :]

    def folded(total):
        return (total[:16] + pltpu.roll(total[16:], RANK, 1))[:, :RANK]

    for h in range(8):
        yy, zz = h // 2, 2 * (h % 2)
        four = jnp.concatenate([block(yy, zz), block(yy, zz + 1)], axis=1)
        top = dot(four, ut_ref[h])
        tops[h] = jnp.concatenate([top[:, :HALF], top[:, HALF:]], axis=0).astype(jnp.bfloat16)
    by_group = jnp.zeros((32, 128), jnp.float32)
    by_top = jnp.zeros((32, 128), jnp.float32)
    for k in range(FAR):
        g = far_src[0, k]
        pair = block(g >> 3, (g >> 1) & 3).astype(jnp.float32)
        turn = (g & 1) * RANK
        halves = [pltpu.roll(pair, turn, 1)[:, :HALF], pltpu.roll(pair, turn + 3 * HALF, 1)[:, :HALF]]
        by_group = by_group + dot(jnp.concatenate(halves, axis=0).astype(jnp.bfloat16), coupling(far_type[0, k]))
        by_top = by_top + dot(tops[top_src[parent, k]], coupling(top_type[parent, k]))
    top_local = folded(by_top).astype(jnp.bfloat16)
    group_local = (folded(by_group) + dot(top_local, dt_ref[group])).astype(jnp.bfloat16)
    mid_local = dot(group_local, dg_ref[...]).astype(jnp.bfloat16)
    for n in range(8):
        out_ref[n * 16 : (n + 1) * 16, :] = dot(mid_local, dn_ref[n]).astype(jnp.bfloat16)


def down_sweep(far_src, far_type, top_src, top_type, columns, up_top, down_top, turned, down_group, down_node):
    smem = pl.BlockSpec(memory_space=pltpu.SMEM)
    vmem = pl.BlockSpec(memory_space=pltpu.VMEM)
    return pl.pallas_call(
        down_kernel,
        in_specs=[smem] * 4 + [vmem] * 9,
        out_specs=vmem,
        out_shape=jax.ShapeDtypeStruct((128, RANK), jnp.bfloat16),
        scratch_shapes=[pltpu.VMEM((256, 128), jnp.bfloat16), pltpu.VMEM((8, 32, HALF), jnp.bfloat16)],
        compiler_params=pltpu.CompilerParams(vmem_limit_bytes=VMEM),
        cost_estimate=pl.CostEstimate(flops=20_000_000, bytes_accessed=5_000_000, transcendentals=0),
        name="down_sweep",
    )(far_src, far_type, top_src, top_type, *columns, up_top, down_top, turned, down_group, down_node)


def far_kernel(
    slot_ref, type_ref, g0, g1, z0, z1, z2, z3, e0, e1, turned_hbm, rows_hbm, down_hbm, near0, near1, node_ref,
    out_ref, table, turned, rows_buf, down_buf, near_buf, found, scalars, sems, scalar_sem,
):
    copies = []
    for j, ref in enumerate((g0, g1, z0, z1, z2, z3)):
        copies.append((ref, table.at[pl.ds(j * 4 * BLOCK, 4 * BLOCK), :]))
    for j, ref in enumerate((e0, e1)):
        copies.append((ref, table.at[pl.ds((24 + j) * BLOCK, BLOCK), :]))
    copies += [(turned_hbm, turned), (down_hbm, down_buf), (rows_hbm, rows_buf)]
    copies += [(near0, near_buf.at[0]), (near1, near_buf.at[1])]
    copies = [pltpu.make_async_copy(source, target, sems.at[j]) for j, (source, target) in enumerate(copies)]
    for c in copies:
        c.start()

    group, x = place()
    core = group & 1
    i_in_block = core * 4 + x

    def slot_of(offset):
        at = i_in_block + offset
        away = at >> 3
        d = (x - at) & 3
        same = jnp.where(((at >> 2) & 1) == core, 0, 4)
        base = jnp.where(away == 0, 0, jnp.where(away < 0, 8, 16))
        inside = base + same + d
        far = jnp.where((offset == 10) | (offset == -10), 24, 25)
        return jnp.where((away > 1) | (away < -1), far, inside)

    found[...] = jnp.zeros_like(found)
    found[:, :LEAVES] = slot_ref[...]
    slots = found[...]
    j_of = (slots * 1366) >> 16
    c_of = slots - j_of * SLOTS
    row_of = slot_of(j_of - 10) * BLOCK
    for c in copies[:8]:
        c.wait()
    leaf = jnp.zeros_like(slots)
    for j in range(OFFSETS):
        row = slot_of(jnp.int32(j - 10)) * BLOCK + TABLE_ROW + (j // 16) * 16
        rows = table[pl.ds(pl.multiple_of(row, 16), 16), :].astype(jnp.float32)
        line = jnp.broadcast_to(rows[j % 16 : j % 16 + 1, :], (8, 128)).astype(jnp.int32)
        here = jnp.take_along_axis(line, c_of, axis=1)
        leaf = jnp.where(j_of == j, here, leaf)
    leaf = leaf & (LEAVES - 1)
    found[...] = (row_of + (leaf >> 2) * 32) * 4 + (leaf & 3)
    to_scalars = pltpu.make_async_copy(found, scalars, scalar_sem)
    to_scalars.start()
    for c in copies[8:]:
        c.wait()
    to_scalars.wait()

    quarter = lane_index(32) // HALF

    def source(k, t):
        code = scalars[k, t]
        block = table[pl.ds(pl.multiple_of(code >> 2, 32), 32), :].astype(jnp.float32)
        return pltpu.roll(block, (((k & 3) - code) & 3) * HALF, 1)

    def left_side(t):
        parts = []
        for m in range(2):
            part = source(4 * m, t)
            for a in range(1, 4):
                part = jnp.where(quarter == a, source(4 * m + a, t), part)
            parts.append(part.astype(jnp.bfloat16))
        return jnp.concatenate(parts, axis=1)

    def right_side(t):
        return jnp.concatenate(
            [turned[pl.ds(pl.multiple_of(type_ref[k, t] * HALF, HALF), HALF), :] for k in range(FAR)], axis=0
        )

    for j in range(2):

        @pl.loop(0, LEAVES // 2, step=16)
        def _(i):
            leaves = [j * (LEAVES // 2) + i + u for u in range(16)]
            lefts = [left_side(t) for t in leaves]
            both = [dot(x, right_side(t)) for x, t in zip(lefts, leaves)]
            nodes = [node_ref[pl.ds(pl.multiple_of((t >> 3) * 16, 16), 16), :] for t in leaves[::8]]
            inherited = [dot(nodes[u // 8], down_buf[t]) for u, t in enumerate(leaves)]
            total = [(p[:16] + pltpu.roll(p[16:], RANK, 1))[:, :RANK] + q for p, q in zip(both, inherited)]
            out = [dot(p.astype(jnp.bfloat16), rows_buf[t]) for p, t in zip(total, leaves)]
            near = near_buf[j, :, pl.ds(pl.multiple_of(i * PANEL, 16 * PANEL), 16 * PANEL)]
            at = pl.multiple_of(leaves[0] * PANEL, 16 * PANEL)
            out_ref[:, pl.ds(at, 16 * PANEL)] = jnp.concatenate(out, axis=1) + near


def far_field(slots, types, pieces, extras, turned, row_basis, down_leaf, near, node_local):
    smem = pl.BlockSpec(memory_space=pltpu.SMEM)
    vmem = pl.BlockSpec(memory_space=pltpu.VMEM)
    hbm = pl.BlockSpec(memory_space=pl.ANY)
    return pl.pallas_call(
        far_kernel,
        in_specs=[vmem, smem] + [hbm] * 13 + [vmem],
        out_specs=vmem,
        out_shape=jax.ShapeDtypeStruct((16, LEAVES * PANEL), jnp.float32),
        scratch_shapes=[
            pltpu.VMEM((26 * BLOCK, 128), jnp.bfloat16),
            pltpu.VMEM((TYPES * HALF, 128), jnp.bfloat16),
            pltpu.VMEM((LEAVES, RANK, PANEL), jnp.bfloat16),
            pltpu.VMEM((LEAVES, RANK, RANK), jnp.bfloat16),
            pltpu.VMEM((2, 16, LEAVES // 2 * PANEL), jnp.float32),
            pltpu.VMEM((8, 128), jnp.int32),
            pltpu.SMEM((8, 128), jnp.int32),
            pltpu.SemaphoreType.DMA((13,)),
            pltpu.SemaphoreType.DMA,
        ],
        compiler_params=pltpu.CompilerParams(vmem_limit_bytes=VMEM),
        cost_estimate=pl.CostEstimate(flops=300_000_000, bytes_accessed=11_000_000, transcendentals=0),
        name="far_field",
    )(slots, types, *pieces, *extras, turned, row_basis, down_leaf, *near, node_local)


def per_device(
    loads,
    col_basis,
    row_basis,
    near_blocks,
    near_src,
    up_leaf,
    down_leaf,
    up_node,
    down_node,
    up_group,
    down_group,
    up_top,
    downward_top_transfer,
    coupling,
    send_table,
    distant_leaf_slot_index,
    far_leaf_type,
    far_group_src,
    far_group_type,
    far_top_src,
    far_top_type,
):
    half = HALO * PANEL
    low = moved(loads[:, half:], line_shift(1))
    high = moved(loads[:, :half], line_shift(-1))

    own = up_sweep(loads, jnp.swapaxes(col_basis, 1, 2), up_leaf, up_node, up_group[0], jnp.swapaxes(send_table, 0, 1))
    along_x = [moved(own, x_shift(d)) for d in (1, 2, 3)]
    extra = [moved(own, two_blocks_away(2, 10)), moved(own, two_blocks_away(1, 9))]
    turned = turned_couplings(jnp.transpose(coupling, (1, 2, 0)).reshape(2, HALF * RANK, TYPES))
    *along_x, low, high, turned = lax.optimization_barrier((*along_x, low, high, turned))

    mine = jnp.concatenate([own] + along_x, axis=0)
    theirs = moved(mine, CORE_SWAP)
    below = moved(mine, line_shift(8))
    above = moved(mine, line_shift(-8))
    pair = group_sums(mine.reshape(4, BLOCK, 128), theirs.reshape(4, BLOCK, 128))
    near0 = near_field(near_src.T, low, loads, high, near_blocks, 0, LEAVES // 2)
    along_y = [moved(pair, y_shift(d)) for d in (1, 2, 3)]
    *along_y, near0 = lax.optimization_barrier((*along_y, near0))
    column = jnp.concatenate([pair] + along_y, axis=0)
    along_z = [moved(column, z_shift(d)) for d in (1, 2, 3)]
    near1 = near_field(near_src.T, low, loads, high, near_blocks, LEAVES // 2, LEAVES // 2)
    *along_z, below, above, near1 = lax.optimization_barrier((*along_z, below, above, near1))
    node_local = down_sweep(
        far_group_src,
        far_group_type,
        far_top_src,
        far_top_type,
        [column] + along_z,
        up_top.reshape(8, 4 * RANK, RANK),
        downward_top_transfer,
        turned,
        down_group[0],
        down_node,
    )
    pieces = [mine, theirs, below, moved(below, CORE_SWAP), above, moved(above, CORE_SWAP)]
    return far_field(
        distant_leaf_slot_index.T,
        far_leaf_type.T,
        pieces,
        extra,
        turned,
        jnp.swapaxes(row_basis, 1, 2),
        down_leaf,
        [near0, near1],
        node_local,
    )


def solution(mesh):
    whole, split = P(), P(AXES)
    return jax.shard_map(
        per_device,
        mesh=mesh,
        in_specs=(
            P(None, AXES),
            split, split, split, split, split, split, split, split, split, split,
            whole, whole, whole,
            split, split, split,
            P("leaf"), P("leaf"),
            whole, whole,
        ),
        out_specs=P(None, AXES),
        check_vma=False,
    )
```

```python
import functools

import jax
import jax.numpy as jnp
from jax import lax
from jax.experimental import pallas as pl
from jax.experimental.pallas import tpu as pltpu
from jax.sharding import PartitionSpec as P

AXES = ("leaf", "sub")
DEVICES = 128
RANK = 64
PANEL = 128
LEAVES = 64
FAR = 8
NEAR = 6
HALO = 32
OFFSETS = 21
SLOTS = 48
TYPES = 316
HALF = 32
TYPE_ROWS = 328
VMEM = 60 << 20
UP_CHUNKS = 2
TERM_ROW = 512
TABLE_ROW = 528
BLOCK = 560
NT = (((1,), (1,)), ((), ()))


def dot(a, b):
    return jnp.dot(a, b, preferred_element_type=jnp.float32)


def dot_nt(a, b):
    return lax.dot_general(a, b, NT, preferred_element_type=jnp.float32)


def lane_index(rows):
    return lax.broadcasted_iota(jnp.int32, (rows, 128), 1)


def place():
    group, sub = lax.axis_index("leaf"), lax.axis_index("sub")
    return group, sub


def moved(value, pairs):
    return lax.ppermute(value, AXES, pairs)


def flipped(bits):
    return [(p, p ^ bits) for p in range(DEVICES)]


def line_swap(step, odd):
    low = [p for p in range(DEVICES - step) if (p // step) % 2 == odd]
    return [(p, p + step) for p in low] + [(p + step, p) for p in low]


CORE_SWAP = flipped(4)


def two_blocks_away():
    pairs = []
    for p in range(DEVICES):
        x, core = p & 3, (p >> 2) & 1
        target = p + 12 if core == 1 else p - 12
        if (x < 2) == (core == 1) and 0 <= target < DEVICES:
            pairs.append((p, target))
    return pairs


def up_kernel(
    x_hbm, cb_hbm, ul_hbm, un_hbm, ug_hbm, table_ref, out_ref, halo0, halo1,
    x_ref, cb_ref, ul_ref, un_ref, ug_ref, lines, sems,
):
    quarter = lane_index(16) // HALF
    per = LEAVES // UP_CHUNKS
    first = [pltpu.make_async_copy(x_hbm, x_ref, sems.at[0])]
    chunks = []
    for j in range(UP_CHUNKS):
        part = pl.ds(j * per, per)
        chunks.append(
            [
                pltpu.make_async_copy(cb_hbm.at[part], cb_ref.at[part], sems.at[3 + j]),
                pltpu.make_async_copy(ul_hbm.at[part], ul_ref.at[part], sems.at[3 + UP_CHUNKS + j]),
            ]
        )
    last = [pltpu.make_async_copy(un_hbm, un_ref, sems.at[1]), pltpu.make_async_copy(ug_hbm, ug_ref, sems.at[2])]
    for c in first + [c for chunk in chunks for c in chunk] + last:
        c.start()
    lines[...] = jnp.zeros_like(lines)
    for j in range(OFFSETS):
        lines[j : j + 1, :SLOTS] = table_ref[j].astype(jnp.float32)
    out_ref[TABLE_ROW:BLOCK, :] = lines[...].astype(jnp.bfloat16)
    first[0].wait()
    lower, upper = x_ref[:, : HALO * PANEL], x_ref[:, HALO * PANEL :]
    odd = jnp.full(lower.shape, place()[1] & 1, jnp.int32) == 1
    halo0[...] = jnp.where(odd, lower, upper)
    halo1[...] = jnp.where(odd, upper, lower)
    nodes = []
    for j in range(UP_CHUNKS):
        for c in chunks[j]:
            c.wait()
        for n in range(j * per // 8, (j + 1) * per // 8):
            node = jnp.zeros((16, RANK), jnp.float32)
            for b in range(2):
                four = range(n * 8 + b * 4, n * 8 + b * 4 + 4)
                x = jnp.concatenate([x_ref[:, t * PANEL : (t + 1) * PANEL] for t in four], axis=0)
                halves = []
                for q in range(2):
                    rows = slice(q * HALF, (q + 1) * HALF)
                    got = dot_nt(x, jnp.concatenate([cb_ref[t, rows, :] for t in four], axis=0))
                    block = got[:16]
                    for a in range(1, 4):
                        block = jnp.where(quarter == a, got[a * 16 : (a + 1) * 16], block)
                    block = block.astype(jnp.bfloat16)
                    halves.append(block)
                    node = node + dot(block, jnp.concatenate([ul_ref[t, rows, :] for t in four], axis=0))
                row = (n * 2 + b) * 32
                out_ref[row : row + 32, :] = jnp.concatenate(halves, axis=0)
            nodes.append(node.astype(jnp.bfloat16))
    for c in last:
        c.wait()
    mid = dot(nodes[0], un_ref[0])
    for n in range(1, len(nodes)):
        mid = mid + dot(nodes[n], un_ref[n])
    term = dot(mid.astype(jnp.bfloat16), ug_ref[...])
    high = term.astype(jnp.bfloat16).astype(jnp.float32)
    parts = jnp.concatenate([high, term - high], axis=1)
    out_ref[TERM_ROW : TERM_ROW + 16, :] = parts.astype(jnp.bfloat16)


def up_sweep(loads, col_basis, up_leaf, up_node, up_group, table):
    vmem = pl.BlockSpec(memory_space=pltpu.VMEM)
    hbm = pl.BlockSpec(memory_space=pl.ANY)
    return pl.pallas_call(
        up_kernel,
        in_specs=[hbm] * 5 + [vmem],
        out_specs=[vmem] * 3,
        out_shape=[jax.ShapeDtypeStruct((BLOCK, 128), jnp.bfloat16)]
        + [jax.ShapeDtypeStruct((16, HALO * PANEL), jnp.bfloat16)] * 2,
        scratch_shapes=[
            pltpu.VMEM((16, LEAVES * PANEL), jnp.bfloat16),
            pltpu.VMEM((LEAVES, RANK, PANEL), jnp.bfloat16),
            pltpu.VMEM((LEAVES, RANK, RANK), jnp.bfloat16),
            pltpu.VMEM((8, RANK, RANK), jnp.bfloat16),
            pltpu.VMEM((RANK, RANK), jnp.bfloat16),
            pltpu.VMEM((32, 128), jnp.float32),
            pltpu.SemaphoreType.DMA((3 + 2 * UP_CHUNKS,)),
        ],
        compiler_params=pltpu.CompilerParams(vmem_limit_bytes=VMEM),
        cost_estimate=pl.CostEstimate(flops=1000, bytes_accessed=1000, transcendentals=0),
        name="up_sweep",
    )(loads, col_basis, up_leaf, up_node, up_group, table)


def turn_kernel(k_ref, out_ref, table):
    step = pl.program_id(0)
    per_step = k_ref.shape[1] // RANK
    for r in range(per_step):
        rows = slice(r * RANK, (r + 1) * RANK)
        both = jnp.concatenate([k_ref[0, rows, :], k_ref[1, rows, :]], axis=0).astype(jnp.float32)
        row = pl.multiple_of((step * per_step + r) * TYPE_ROWS, 8)
        table[pl.ds(row, TYPES), :] = both.T

    @pl.when(step == pl.num_programs(0) - 1)
    def _():
        @pl.loop(0, TYPES // 4)
        def _(i):
            for u in range(4):
                t = i * 4 + u
                matrix = table[pl.ds(t, HALF, stride=TYPE_ROWS), :].astype(jnp.bfloat16)
                out_ref[pl.ds(pl.multiple_of(t * HALF, HALF), HALF), :] = matrix


def turned_couplings(coupling):
    steps = 4
    rows = TYPES * HALF
    return pl.pallas_call(
        turn_kernel,
        grid=(steps,),
        in_specs=[pl.BlockSpec((2, HALF * RANK // steps, TYPES), lambda i: (0, i, 0))],
        out_specs=pl.BlockSpec((rows, 128), lambda i: (0, 0)),
        out_shape=jax.ShapeDtypeStruct((rows, 128), jnp.bfloat16),
        scratch_shapes=[pltpu.VMEM((HALF * TYPE_ROWS, 128), jnp.float32)],
        compiler_params=pltpu.CompilerParams(vmem_limit_bytes=16 << 20),
        cost_estimate=pl.CostEstimate(flops=1000, bytes_accessed=1000, transcendentals=0),
        name="turn_couplings",
    )(coupling)


def near_kernel(first, src, halo0, own_ref, halo1, blocks_hbm, out_ref, all_x, blocks, sems):
    chunks = sems.shape[0]
    count = blocks.shape[0]
    per = count // chunks

    def copy(j):
        return pltpu.make_async_copy(
            blocks_hbm.at[pl.ds(first + j * per, per)], blocks.at[pl.ds(j * per, per)], sems.at[j]
        )

    for j in range(chunks):
        copy(j).start()
    group, sub = place()
    one, two = halo0[...], halo1[...]
    odd = jnp.full(one.shape, sub & 1, jnp.int32) == 1
    all_x[:, : HALO * PANEL] = jnp.where(odd, one, two)
    all_x[:, HALO * PANEL : (HALO + LEAVES) * PANEL] = own_ref[...]
    all_x[:, (HALO + LEAVES) * PANEL :] = jnp.where(odd, two, one)
    start = (group * 4 + sub) * LEAVES - HALO

    @pl.loop(0, chunks)
    def _(j):
        copy(j).wait()
        out = []
        for u in range(per):
            t = j * per + u
            x = []
            for k in range(NEAR):
                i = src[k, first + t] - start
                x.append(all_x[:, pl.ds(pl.multiple_of(i * PANEL, PANEL), PANEL)])
            row = jnp.concatenate([blocks[t, k] for k in range(NEAR)], axis=1)
            out.append(dot_nt(jnp.concatenate(x, axis=1), row))
        at = pl.multiple_of(j * (per * PANEL), per * PANEL)
        out_ref[:, pl.ds(at, per * PANEL)] = jnp.concatenate(out, axis=1)


def near_field(src, halo0, own, halo1, blocks, first, count):
    chunks = 4
    vmem = pl.BlockSpec(memory_space=pltpu.VMEM)
    return pl.pallas_call(
        functools.partial(near_kernel, first),
        in_specs=[pl.BlockSpec(memory_space=pltpu.SMEM), vmem, vmem, vmem, pl.BlockSpec(memory_space=pl.ANY)],
        out_specs=vmem,
        out_shape=jax.ShapeDtypeStruct((16, count * PANEL), jnp.float32),
        scratch_shapes=[
            pltpu.VMEM((16, (2 * HALO + LEAVES) * PANEL), jnp.bfloat16),
            pltpu.VMEM((count, NEAR, PANEL, PANEL), jnp.bfloat16),
            pltpu.SemaphoreType.DMA((chunks,)),
        ],
        compiler_params=pltpu.CompilerParams(vmem_limit_bytes=60 << 20),
        cost_estimate=pl.CostEstimate(flops=1000, bytes_accessed=1000, transcendentals=0),
        name="near_field",
    )(src, halo0, own, halo1, blocks)


def join_kernel(own, x1, x2, x3, mine_ref, group_ref):
    total = jnp.zeros((16, 128), jnp.float32)
    for d, ref in enumerate((own, x1, x2, x3)):
        mine_ref[d * BLOCK : (d + 1) * BLOCK, :] = ref[...]
        total = total + ref[TERM_ROW : TERM_ROW + 16, :].astype(jnp.float32)
    group_ref[...] = (total + pltpu.roll(total, RANK, 1)).astype(jnp.bfloat16)


def joined(*blocks):
    vmem = pl.BlockSpec(memory_space=pltpu.VMEM)
    return pl.pallas_call(
        join_kernel,
        in_specs=[vmem] * 4,
        out_specs=[vmem] * 2,
        out_shape=[
            jax.ShapeDtypeStruct((4 * BLOCK, 128), jnp.bfloat16),
            jax.ShapeDtypeStruct((16, 128), jnp.bfloat16),
        ],
        compiler_params=pltpu.CompilerParams(vmem_limit_bytes=8 << 20),
        cost_estimate=pl.CostEstimate(flops=1000, bytes_accessed=1000, transcendentals=0),
        name="join_blocks",
    )(*blocks)


def down_kernel(
    far_src, far_type, top_src, top_type, c0, c1, other_core, ut_ref, dt_ref, turned_ref, dg_ref, dn_ref, out_ref,
    groups, tops, couplings, own_dt, sems,
):
    group, _ = place()
    y, z, parent = group >> 3, (group >> 1) & 3, group >> 2
    left = lax.broadcasted_iota(jnp.int32, (128, 128), 1) < RANK
    first_core = jnp.full((128, 128), group & 1, jnp.int32) == 0
    for j, ref in enumerate((c0, c1)):
        rows = slice(j * 128, (j + 1) * 128)
        groups[rows, :] = jnp.where(left == first_core, ref[...], other_core[rows, :])

    def block(yy, zz):
        at = (y ^ yy) * 4 + (z ^ zz)
        return groups[pl.ds(pl.multiple_of(at * 16, 16), 16), :]

    kinds = [far_type[0, k] for k in range(FAR)] + [top_type[parent, k] for k in range(FAR)]
    copies = [
        pltpu.make_async_copy(
            turned_ref.at[pl.ds(pl.multiple_of(kind * HALF, HALF), HALF), :],
            couplings.at[pl.ds(j * HALF, HALF), :],
            sems.at[j],
        )
        for j, kind in enumerate(kinds)
    ]
    copies.append(pltpu.make_async_copy(dt_ref.at[group], own_dt, sems.at[2 * FAR]))
    for c in copies:
        c.start()

    def coupling(j):
        return couplings[j * HALF : (j + 1) * HALF, :]

    def folded(total):
        return (total[:16] + pltpu.roll(total[16:], RANK, 1))[:, :RANK]

    for h in range(8):
        yy, zz = h // 2, 2 * (h % 2)
        four = jnp.concatenate([block(yy, zz), block(yy, zz + 1)], axis=1)
        top = dot(four, ut_ref[h])
        tops[h] = jnp.concatenate([top[:, :HALF], top[:, HALF:]], axis=0).astype(jnp.bfloat16)
    for c in copies:
        c.wait()
    by_group = jnp.zeros((32, 128), jnp.float32)
    by_top = jnp.zeros((32, 128), jnp.float32)
    for k in range(FAR):
        g = far_src[0, k]
        pair = block(g >> 3, (g >> 1) & 3).astype(jnp.float32)
        turn = (g & 1) * RANK
        halves = [pltpu.roll(pair, turn, 1)[:, :HALF], pltpu.roll(pair, turn + 3 * HALF, 1)[:, :HALF]]
        by_group = by_group + dot(jnp.concatenate(halves, axis=0).astype(jnp.bfloat16), coupling(k))
        by_top = by_top + dot(tops[top_src[parent, k]], coupling(FAR + k))
    top_local = folded(by_top).astype(jnp.bfloat16)
    group_local = (folded(by_group) + dot(top_local, own_dt[...])).astype(jnp.bfloat16)
    mid_local = dot(group_local, dg_ref[...]).astype(jnp.bfloat16)
    for n in range(8):
        out_ref[n * 16 : (n + 1) * 16, :] = dot(mid_local, dn_ref[n]).astype(jnp.bfloat16)


def down_sweep(far_src, far_type, top_src, top_type, groups, up_top, down_top, turned, down_group, down_node):
    smem = pl.BlockSpec(memory_space=pltpu.SMEM)
    vmem = pl.BlockSpec(memory_space=pltpu.VMEM)
    hbm = pl.BlockSpec(memory_space=pl.ANY)
    return pl.pallas_call(
        down_kernel,
        in_specs=[smem] * 4 + [vmem] * 4 + [hbm] * 2 + [vmem] * 2,
        out_specs=vmem,
        out_shape=jax.ShapeDtypeStruct((128, RANK), jnp.bfloat16),
        scratch_shapes=[
            pltpu.VMEM((256, 128), jnp.bfloat16),
            pltpu.VMEM((8, 32, HALF), jnp.bfloat16),
            pltpu.VMEM((2 * FAR * HALF, 128), jnp.bfloat16),
            pltpu.VMEM((RANK, RANK), jnp.bfloat16),
            pltpu.SemaphoreType.DMA((2 * FAR + 1,)),
        ],
        compiler_params=pltpu.CompilerParams(vmem_limit_bytes=8 << 20),
        cost_estimate=pl.CostEstimate(flops=1000, bytes_accessed=1000, transcendentals=0),
        name="down_sweep",
    )(far_src, far_type, top_src, top_type, *groups, up_top, down_top, turned, down_group, down_node)


def far_kernel(
    slot_ref, type_ref, g0, g1, z0, z1, z2, z3, e0, turned, rows_buf, down_buf, near0, near1, node_ref,
    out_ref, table, found, scalars, sems, scalar_sem,
):
    copies = []
    for j, ref in enumerate((g0, g1, z0, z1, z2, z3)):
        copies.append((ref, table.at[pl.ds(j * 4 * BLOCK, 4 * BLOCK), :]))
    copies.append((e0, table.at[pl.ds(24 * BLOCK, 2 * BLOCK), :]))
    copies = [pltpu.make_async_copy(source, target, sems.at[j]) for j, (source, target) in enumerate(copies)]
    for c in copies:
        c.start()

    group, x = place()
    core, block = group & 1, group >> 1
    i_in_block = core * 4 + x

    def slot_of(offset):
        at = i_in_block + offset
        away = at >> 3
        d = (x ^ at) & 3
        same = jnp.where(((at >> 2) & 1) == core, 0, 4)
        first = jnp.where((block & 1) == 0, 1, -1)
        base = jnp.where(away == 0, 0, jnp.where(away == first, 8, 16))
        inside = base + same + d
        return jnp.where((away > 1) | (away < -1), 22 + d, inside)

    found[...] = jnp.zeros_like(found)
    found[:, :LEAVES] = slot_ref[...]
    slots = found[...]
    j_of = (slots * 1366) >> 16
    c_of = slots - j_of * SLOTS
    row_of = slot_of(j_of - 10) * BLOCK
    for c in copies:
        c.wait()
    leaf = jnp.zeros_like(slots)
    for j in range(OFFSETS):
        row = slot_of(jnp.int32(j - 10)) * BLOCK + TABLE_ROW + (j // 16) * 16
        rows = table[pl.ds(pl.multiple_of(row, 16), 16), :].astype(jnp.float32)
        line = jnp.broadcast_to(rows[j % 16 : j % 16 + 1, :], (8, 128)).astype(jnp.int32)
        here = jnp.take_along_axis(line, c_of, axis=1)
        leaf = jnp.where(j_of == j, here, leaf)
    leaf = leaf & (LEAVES - 1)
    found[...] = (row_of + (leaf >> 2) * 32) * 4 + (leaf & 3)
    to_scalars = pltpu.make_async_copy(found, scalars, scalar_sem)
    to_scalars.start()
    to_scalars.wait()

    quarter = lane_index(32) // HALF

    def source(k, t):
        code = scalars[k, t]
        block = table[pl.ds(pl.multiple_of(code >> 2, 32), 32), :].astype(jnp.float32)
        return pltpu.roll(block, (((k & 3) - code) & 3) * HALF, 1)

    def left_side(t):
        parts = []
        for m in range(2):
            part = source(4 * m, t)
            for a in range(1, 4):
                part = jnp.where(quarter == a, source(4 * m + a, t), part)
            parts.append(part.astype(jnp.bfloat16))
        return jnp.concatenate(parts, axis=1)

    def right_side(t):
        return jnp.concatenate(
            [turned[pl.ds(pl.multiple_of(type_ref[k, t] * HALF, HALF), HALF), :] for k in range(FAR)], axis=0
        )

    for j, near_ref in enumerate((near0, near1)):

        @pl.loop(0, LEAVES // 2, step=16)
        def _(i):
            leaves = [j * (LEAVES // 2) + i + u for u in range(16)]
            lefts = [left_side(t) for t in leaves]
            both = [dot(x, right_side(t)) for x, t in zip(lefts, leaves)]
            nodes = [node_ref[pl.ds(pl.multiple_of((t >> 3) * 16, 16), 16), :] for t in leaves[::8]]
            inherited = [dot(nodes[u // 8], down_buf[t]) for u, t in enumerate(leaves)]
            total = [(p[:16] + pltpu.roll(p[16:], RANK, 1))[:, :RANK] + q for p, q in zip(both, inherited)]
            out = [dot(p.astype(jnp.bfloat16), rows_buf[t]) for p, t in zip(total, leaves)]
            near = near_ref[:, pl.ds(pl.multiple_of(i * PANEL, 16 * PANEL), 16 * PANEL)]
            at = pl.multiple_of(leaves[0] * PANEL, 16 * PANEL)
            out_ref[:, pl.ds(at, 16 * PANEL)] = jnp.concatenate(out, axis=1) + near


def far_field(slots, types, pieces, extra, turned, row_basis, down_leaf, near, node_local):
    smem = pl.BlockSpec(memory_space=pltpu.SMEM)
    vmem = pl.BlockSpec(memory_space=pltpu.VMEM)
    hbm = pl.BlockSpec(memory_space=pl.ANY)
    return pl.pallas_call(
        far_kernel,
        in_specs=[vmem, smem] + [hbm] * 7 + [vmem] * 6,
        out_specs=vmem,
        out_shape=jax.ShapeDtypeStruct((16, LEAVES * PANEL), jnp.float32),
        scratch_shapes=[
            pltpu.VMEM((26 * BLOCK, 128), jnp.bfloat16),
            pltpu.VMEM((8, 128), jnp.int32),
            pltpu.SMEM((8, 128), jnp.int32),
            pltpu.SemaphoreType.DMA((7,)),
            pltpu.SemaphoreType.DMA,
        ],
        compiler_params=pltpu.CompilerParams(vmem_limit_bytes=16 << 20),
        cost_estimate=pl.CostEstimate(flops=1000, bytes_accessed=1000, transcendentals=0),
        name="far_field",
    )(slots, types, *pieces, extra, turned, row_basis, down_leaf, *near, node_local)


def per_device(
    loads,
    col_basis,
    row_basis,
    near_blocks,
    near_src,
    up_leaf,
    down_leaf,
    up_node,
    down_node,
    up_group,
    down_group,
    up_top,
    downward_top_transfer,
    coupling,
    send_table,
    distant_leaf_slot_index,
    far_leaf_type,
    far_group_src,
    far_group_type,
    far_top_src,
    far_top_type,
):
    own, to_first, to_second = up_sweep(
        loads, jnp.swapaxes(col_basis, 1, 2), up_leaf, up_node, up_group[0], jnp.swapaxes(send_table, 0, 1)
    )
    along_x = {d: moved(own, flipped(d)) for d in (3, 1, 2)}
    halo0, halo1 = moved(to_first, line_swap(1, 0)), moved(to_second, line_swap(1, 1))
    x1, x2, x3, halo0, halo1, coupling = lax.optimization_barrier(
        (along_x[1], along_x[2], along_x[3], halo0, halo1, coupling)
    )
    mine, group = joined(own, x1, x2, x3)
    along_z = [moved(group, flipped(8 * d)) for d in (1, 2, 3)]
    *along_z, mine = lax.optimization_barrier((*along_z, mine))
    theirs = moved(mine, CORE_SWAP)
    extra = moved(mine[2 * BLOCK :], two_blocks_away())
    z0, z1 = moved(mine, line_swap(8, 0)), moved(mine, line_swap(8, 1))
    column = jnp.concatenate([group] + along_z)
    y1 = moved(column, flipped(32))
    theirs, halo0, halo1, coupling = lax.optimization_barrier((theirs, halo0, halo1, coupling))
    near0 = near_field(near_src.T, halo0, loads, halo1, near_blocks, 0, LEAVES // 2)
    y1, near0, halo0 = lax.optimization_barrier((y1, near0, halo0))
    column = jnp.concatenate([column, y1])
    y2 = moved(column, flipped(64))
    near1 = near_field(near_src.T, halo0, loads, halo1, near_blocks, LEAVES // 2, LEAVES // 2)
    y2, near1, coupling = lax.optimization_barrier((y2, near1, coupling))
    turned = turned_couplings(jnp.transpose(coupling, (1, 2, 0)).reshape(2, HALF * RANK, TYPES))
    y2, turned, z0, z1, extra = lax.optimization_barrier((y2, turned, z0, z1, extra))
    other_core = moved(jnp.concatenate([column, y2]), CORE_SWAP)
    swapped = [moved(z0, CORE_SWAP), moved(z1, CORE_SWAP)]
    node_local = down_sweep(
        far_group_src,
        far_group_type,
        far_top_src,
        far_top_type,
        [column, y2, other_core],
        up_top.reshape(8, 4 * RANK, RANK),
        downward_top_transfer,
        turned,
        down_group[0],
        down_node,
    )
    pieces = [mine, theirs, z0, swapped[0], z1, swapped[1]]
    return far_field(
        distant_leaf_slot_index.T,
        far_leaf_type.T,
        pieces,
        extra,
        turned,
        jnp.swapaxes(row_basis, 1, 2),
        down_leaf,
        [near0, near1],
        node_local,
    )


def solution(mesh):
    whole, split = P(), P(AXES)
    return jax.shard_map(
        per_device,
        mesh=mesh,
        in_specs=(
            P(None, AXES),
            split, split, split, split, split, split, split, split, split, split,
            whole, whole, whole,
            split, split, split,
            P("leaf"), P("leaf"),
            whole, whole,
        ),
        out_specs=P(None, AXES),
        check_vma=False,
    )
```

```python
import functools

import jax
import jax.numpy as jnp
from jax import lax
from jax.experimental import pallas as pl
from jax.experimental.pallas import tpu as pltpu
from jax.sharding import PartitionSpec as P

AXES = ("leaf", "sub")
DEVICES = 128
RANK = 64
PANEL = 128
LEAVES = 64
FAR = 8
NEAR = 6
HALO = 32
OFFSETS = 21
SLOTS = 48
TYPES = 316
HALF = 32
TYPE_ROWS = 328
VMEM = 60 << 20
UP_CHUNKS = 2
TERM_ROW = 512
TABLE_ROW = 528
BLOCK = 560
NT = (((1,), (1,)), ((), ()))


def dot(a, b):
    return jnp.dot(a, b, preferred_element_type=jnp.float32)


def dot_nt(a, b):
    return lax.dot_general(a, b, NT, preferred_element_type=jnp.float32)


def lane_index(rows):
    return lax.broadcasted_iota(jnp.int32, (rows, 128), 1)


def place():
    group, sub = lax.axis_index("leaf"), lax.axis_index("sub")
    return group, sub


def moved(value, pairs):
    return lax.ppermute(value, AXES, pairs)


def flipped(bits):
    return [(p, p ^ bits) for p in range(DEVICES)]


def line_swap(step, odd):
    low = [p for p in range(DEVICES - step) if (p // step) % 2 == odd]
    return [(p, p + step) for p in low] + [(p + step, p) for p in low]


CORE_SWAP = flipped(4)


def two_blocks_away():
    pairs = []
    for p in range(DEVICES):
        x, core = p & 3, (p >> 2) & 1
        target = p + 12 if core == 1 else p - 12
        if (x < 2) == (core == 1) and 0 <= target < DEVICES:
            pairs.append((p, target))
    return pairs


def up_kernel(
    x_hbm, cb_hbm, ul_hbm, un_hbm, ug_hbm, table_ref, out_ref, halo0, halo1,
    x_ref, cb_ref, ul_ref, un_ref, ug_ref, lines, sems,
):
    quarter = lane_index(16) // HALF
    per = LEAVES // UP_CHUNKS
    first = [pltpu.make_async_copy(x_hbm, x_ref, sems.at[0])]
    chunks = []
    for j in range(UP_CHUNKS):
        part = pl.ds(j * per, per)
        chunks.append(
            [
                pltpu.make_async_copy(cb_hbm.at[part], cb_ref.at[part], sems.at[3 + j]),
                pltpu.make_async_copy(ul_hbm.at[part], ul_ref.at[part], sems.at[3 + UP_CHUNKS + j]),
            ]
        )
    last = [pltpu.make_async_copy(un_hbm, un_ref, sems.at[1]), pltpu.make_async_copy(ug_hbm, ug_ref, sems.at[2])]
    for c in first + [c for chunk in chunks for c in chunk] + last:
        c.start()
    lines[...] = jnp.zeros_like(lines)
    for j in range(OFFSETS):
        lines[j : j + 1, :SLOTS] = table_ref[j].astype(jnp.float32)
    out_ref[TABLE_ROW:BLOCK, :] = lines[...].astype(jnp.bfloat16)
    first[0].wait()
    lower, upper = x_ref[:, : HALO * PANEL], x_ref[:, HALO * PANEL :]
    odd = jnp.full(lower.shape, place()[1] & 1, jnp.int32) == 1
    halo0[...] = jnp.where(odd, lower, upper)
    halo1[...] = jnp.where(odd, upper, lower)
    nodes = []
    for j in range(UP_CHUNKS):
        for c in chunks[j]:
            c.wait()
        for n in range(j * per // 8, (j + 1) * per // 8):
            node = jnp.zeros((16, RANK), jnp.float32)
            for b in range(2):
                four = range(n * 8 + b * 4, n * 8 + b * 4 + 4)
                x = jnp.concatenate([x_ref[:, t * PANEL : (t + 1) * PANEL] for t in four], axis=0)
                halves = []
                for q in range(2):
                    rows = slice(q * HALF, (q + 1) * HALF)
                    got = dot_nt(x, jnp.concatenate([cb_ref[t, rows, :] for t in four], axis=0))
                    block = got[:16]
                    for a in range(1, 4):
                        block = jnp.where(quarter == a, got[a * 16 : (a + 1) * 16], block)
                    block = block.astype(jnp.bfloat16)
                    halves.append(block)
                    node = node + dot(block, jnp.concatenate([ul_ref[t, rows, :] for t in four], axis=0))
                row = (n * 2 + b) * 32
                out_ref[row : row + 32, :] = jnp.concatenate(halves, axis=0)
            nodes.append(node.astype(jnp.bfloat16))
    for c in last:
        c.wait()
    mid = dot(nodes[0], un_ref[0])
    for n in range(1, len(nodes)):
        mid = mid + dot(nodes[n], un_ref[n])
    term = dot(mid.astype(jnp.bfloat16), ug_ref[...])
    high = term.astype(jnp.bfloat16).astype(jnp.float32)
    parts = jnp.concatenate([high, term - high], axis=1)
    out_ref[TERM_ROW : TERM_ROW + 16, :] = parts.astype(jnp.bfloat16)


def up_sweep(loads, col_basis, up_leaf, up_node, up_group, table):
    vmem = pl.BlockSpec(memory_space=pltpu.VMEM)
    hbm = pl.BlockSpec(memory_space=pl.ANY)
    return pl.pallas_call(
        up_kernel,
        in_specs=[hbm] * 5 + [vmem],
        out_specs=[vmem] * 3,
        out_shape=[jax.ShapeDtypeStruct((BLOCK, 128), jnp.bfloat16)]
        + [jax.ShapeDtypeStruct((16, HALO * PANEL), jnp.bfloat16)] * 2,
        scratch_shapes=[
            pltpu.VMEM((16, LEAVES * PANEL), jnp.bfloat16),
            pltpu.VMEM((LEAVES, RANK, PANEL), jnp.bfloat16),
            pltpu.VMEM((LEAVES, RANK, RANK), jnp.bfloat16),
            pltpu.VMEM((8, RANK, RANK), jnp.bfloat16),
            pltpu.VMEM((RANK, RANK), jnp.bfloat16),
            pltpu.VMEM((32, 128), jnp.float32),
            pltpu.SemaphoreType.DMA((3 + 2 * UP_CHUNKS,)),
        ],
        compiler_params=pltpu.CompilerParams(vmem_limit_bytes=VMEM),
        cost_estimate=pl.CostEstimate(flops=1000, bytes_accessed=1000, transcendentals=0),
        name="up_sweep",
    )(loads, col_basis, up_leaf, up_node, up_group, table)


def turn_kernel(k_ref, out_ref, table):
    step = pl.program_id(0)
    per_step = k_ref.shape[1] // RANK
    for r in range(per_step):
        rows = slice(r * RANK, (r + 1) * RANK)
        both = jnp.concatenate([k_ref[0, rows, :], k_ref[1, rows, :]], axis=0).astype(jnp.float32)
        row = pl.multiple_of((step * per_step + r) * TYPE_ROWS, 8)
        table[pl.ds(row, TYPES), :] = both.T

    @pl.when(step == pl.num_programs(0) - 1)
    def _():
        @pl.loop(0, TYPES // 4)
        def _(i):
            for u in range(4):
                t = i * 4 + u
                matrix = table[pl.ds(t, HALF, stride=TYPE_ROWS), :].astype(jnp.bfloat16)
                out_ref[pl.ds(pl.multiple_of(t * HALF, HALF), HALF), :] = matrix


def turned_couplings(coupling):
    steps = 4
    rows = TYPES * HALF
    return pl.pallas_call(
        turn_kernel,
        grid=(steps,),
        in_specs=[pl.BlockSpec((2, HALF * RANK // steps, TYPES), lambda i: (0, i, 0))],
        out_specs=pl.BlockSpec((rows, 128), lambda i: (0, 0)),
        out_shape=jax.ShapeDtypeStruct((rows, 128), jnp.bfloat16),
        scratch_shapes=[pltpu.VMEM((HALF * TYPE_ROWS, 128), jnp.float32)],
        compiler_params=pltpu.CompilerParams(vmem_limit_bytes=16 << 20),
        cost_estimate=pl.CostEstimate(flops=1000, bytes_accessed=1000, transcendentals=0),
        name="turn_couplings",
    )(coupling)


def near_kernel(first, src, halo0, own_ref, halo1, blocks_hbm, out_ref, all_x, blocks, sems):
    chunks = sems.shape[0]
    count = blocks.shape[0]
    per = count // chunks

    def copy(j):
        return pltpu.make_async_copy(
            blocks_hbm.at[pl.ds(first + j * per, per)], blocks.at[pl.ds(j * per, per)], sems.at[j]
        )

    for j in range(chunks):
        copy(j).start()
    group, sub = place()
    one, two = halo0[...], halo1[...]
    odd = jnp.full(one.shape, sub & 1, jnp.int32) == 1
    all_x[:, : HALO * PANEL] = jnp.where(odd, one, two)
    all_x[:, HALO * PANEL : (HALO + LEAVES) * PANEL] = own_ref[...]
    all_x[:, (HALO + LEAVES) * PANEL :] = jnp.where(odd, two, one)
    start = (group * 4 + sub) * LEAVES - HALO

    @pl.loop(0, chunks)
    def _(j):
        copy(j).wait()
        out = []
        for u in range(per):
            t = j * per + u
            x = []
            for k in range(NEAR):
                i = src[k, first + t] - start
                x.append(all_x[:, pl.ds(pl.multiple_of(i * PANEL, PANEL), PANEL)])
            row = jnp.concatenate([blocks[t, k] for k in range(NEAR)], axis=1)
            out.append(dot_nt(jnp.concatenate(x, axis=1), row))
        at = pl.multiple_of(j * (per * PANEL), per * PANEL)
        out_ref[:, pl.ds(at, per * PANEL)] = jnp.concatenate(out, axis=1)


def near_field(src, halo0, own, halo1, blocks, first, count):
    chunks = 4
    vmem = pl.BlockSpec(memory_space=pltpu.VMEM)
    return pl.pallas_call(
        functools.partial(near_kernel, first),
        in_specs=[pl.BlockSpec(memory_space=pltpu.SMEM), vmem, vmem, vmem, pl.BlockSpec(memory_space=pl.ANY)],
        out_specs=vmem,
        out_shape=jax.ShapeDtypeStruct((16, count * PANEL), jnp.float32),
        scratch_shapes=[
            pltpu.VMEM((16, (2 * HALO + LEAVES) * PANEL), jnp.bfloat16),
            pltpu.VMEM((count, NEAR, PANEL, PANEL), jnp.bfloat16),
            pltpu.SemaphoreType.DMA((chunks,)),
        ],
        compiler_params=pltpu.CompilerParams(vmem_limit_bytes=52 << 20),
        cost_estimate=pl.CostEstimate(flops=1000, bytes_accessed=1000, transcendentals=0),
        name="near_field",
    )(src, halo0, own, halo1, blocks)


def join_kernel(own, x1, x2, x3, mine_ref, group_ref, tail_ref):
    total = jnp.zeros((16, 128), jnp.float32)
    for d, ref in enumerate((own, x1, x2, x3)):
        mine_ref[d * BLOCK : (d + 1) * BLOCK, :] = ref[...]
        if d >= 2:
            tail_ref[(d - 2) * BLOCK : (d - 1) * BLOCK, :] = ref[...]
        total = total + ref[TERM_ROW : TERM_ROW + 16, :].astype(jnp.float32)
    group_ref[...] = (total + pltpu.roll(total, RANK, 1)).astype(jnp.bfloat16)


def joined(*blocks):
    vmem = pl.BlockSpec(memory_space=pltpu.VMEM)
    return pl.pallas_call(
        join_kernel,
        in_specs=[vmem] * 4,
        out_specs=[vmem] * 3,
        out_shape=[
            jax.ShapeDtypeStruct((4 * BLOCK, 128), jnp.bfloat16),
            jax.ShapeDtypeStruct((16, 128), jnp.bfloat16),
            jax.ShapeDtypeStruct((2 * BLOCK, 128), jnp.bfloat16),
        ],
        compiler_params=pltpu.CompilerParams(vmem_limit_bytes=8 << 20),
        cost_estimate=pl.CostEstimate(flops=1000, bytes_accessed=1000, transcendentals=0),
        name="join_blocks",
    )(*blocks)


def down_kernel(
    far_src, far_type, top_src, top_type, c0, c1, ut_ref, dt_ref, turned_ref, dg_ref, dn_ref, out_ref,
    groups, tops, couplings, own_dt, sems,
):
    group, _ = place()
    y, z, parent = group >> 3, (group >> 1) & 3, group >> 2
    left = lax.broadcasted_iota(jnp.int32, (64, 128), 1) < RANK
    first_core = jnp.full((64, 128), group & 1, jnp.int32) == 0
    for j in range(4):
        ref = (c0, c1)[j // 2]
        at = (j % 2) * 128
        own, other = ref[at : at + 64, :], ref[at + 64 : at + 128, :]
        groups[j * 64 : (j + 1) * 64, :] = jnp.where(left == first_core, own, other)

    def block(yy, zz):
        at = (y ^ yy) * 4 + (z ^ zz)
        return groups[pl.ds(pl.multiple_of(at * 16, 16), 16), :]

    kinds = [far_type[0, k] for k in range(FAR)] + [top_type[parent, k] for k in range(FAR)]
    copies = [
        pltpu.make_async_copy(
            turned_ref.at[pl.ds(pl.multiple_of(kind * HALF, HALF), HALF), :],
            couplings.at[pl.ds(j * HALF, HALF), :],
            sems.at[j],
        )
        for j, kind in enumerate(kinds)
    ]
    copies.append(pltpu.make_async_copy(dt_ref.at[group], own_dt, sems.at[2 * FAR]))
    for c in copies:
        c.start()

    def coupling(j):
        return couplings[j * HALF : (j + 1) * HALF, :]

    def folded(total):
        return (total[:16] + pltpu.roll(total[16:], RANK, 1))[:, :RANK]

    for h in range(8):
        yy, zz = h // 2, 2 * (h % 2)
        four = jnp.concatenate([block(yy, zz), block(yy, zz + 1)], axis=1)
        top = dot(four, ut_ref[h])
        tops[h] = jnp.concatenate([top[:, :HALF], top[:, HALF:]], axis=0).astype(jnp.bfloat16)
    for c in copies:
        c.wait()
    by_group = jnp.zeros((32, 128), jnp.float32)
    by_top = jnp.zeros((32, 128), jnp.float32)
    for k in range(FAR):
        g = far_src[0, k]
        pair = block(g >> 3, (g >> 1) & 3).astype(jnp.float32)
        turn = (g & 1) * RANK
        halves = [pltpu.roll(pair, turn, 1)[:, :HALF], pltpu.roll(pair, turn + 3 * HALF, 1)[:, :HALF]]
        by_group = by_group + dot(jnp.concatenate(halves, axis=0).astype(jnp.bfloat16), coupling(k))
        by_top = by_top + dot(tops[top_src[parent, k]], coupling(FAR + k))
    top_local = folded(by_top).astype(jnp.bfloat16)
    group_local = (folded(by_group) + dot(top_local, own_dt[...])).astype(jnp.bfloat16)
    mid_local = dot(group_local, dg_ref[...]).astype(jnp.bfloat16)
    for n in range(8):
        out_ref[n * 16 : (n + 1) * 16, :] = dot(mid_local, dn_ref[n]).astype(jnp.bfloat16)


def down_sweep(far_src, far_type, top_src, top_type, groups, up_top, down_top, turned, down_group, down_node):
    smem = pl.BlockSpec(memory_space=pltpu.SMEM)
    vmem = pl.BlockSpec(memory_space=pltpu.VMEM)
    hbm = pl.BlockSpec(memory_space=pl.ANY)
    return pl.pallas_call(
        down_kernel,
        in_specs=[smem] * 4 + [vmem] * 3 + [hbm] * 2 + [vmem] * 2,
        out_specs=vmem,
        out_shape=jax.ShapeDtypeStruct((128, RANK), jnp.bfloat16),
        scratch_shapes=[
            pltpu.VMEM((256, 128), jnp.bfloat16),
            pltpu.VMEM((8, 32, HALF), jnp.bfloat16),
            pltpu.VMEM((2 * FAR * HALF, 128), jnp.bfloat16),
            pltpu.VMEM((RANK, RANK), jnp.bfloat16),
            pltpu.SemaphoreType.DMA((2 * FAR + 1,)),
        ],
        compiler_params=pltpu.CompilerParams(vmem_limit_bytes=8 << 20),
        cost_estimate=pl.CostEstimate(flops=1000, bytes_accessed=1000, transcendentals=0),
        name="down_sweep",
    )(far_src, far_type, top_src, top_type, *groups, up_top, down_top, turned, down_group, down_node)


def far_kernel(
    slot_ref, type_ref, g0, g1, z0, z1, z2, z3, e0, turned, rows_buf, down_buf, near0, near1, node_ref,
    out_ref, table, found, scalars, sems, scalar_sem,
):
    copies = []
    for j, ref in enumerate((g0, g1, z0, z1, z2, z3)):
        copies.append((ref, table.at[pl.ds(j * 4 * BLOCK, 4 * BLOCK), :]))
    copies.append((e0, table.at[pl.ds(24 * BLOCK, 2 * BLOCK), :]))
    copies = [pltpu.make_async_copy(source, target, sems.at[j]) for j, (source, target) in enumerate(copies)]
    for c in copies:
        c.start()

    group, x = place()
    core, block = group & 1, group >> 1
    i_in_block = core * 4 + x

    def slot_of(offset):
        at = i_in_block + offset
        away = at >> 3
        d = (x ^ at) & 3
        same = jnp.where(((at >> 2) & 1) == core, 0, 4)
        first = jnp.where((block & 1) == 0, 1, -1)
        base = jnp.where(away == 0, 0, jnp.where(away == first, 8, 16))
        inside = base + same + d
        return jnp.where((away > 1) | (away < -1), 22 + d, inside)

    found[...] = jnp.zeros_like(found)
    found[:, :LEAVES] = slot_ref[...]
    slots = found[...]
    j_of = (slots * 1366) >> 16
    c_of = slots - j_of * SLOTS
    row_of = slot_of(j_of - 10) * BLOCK
    for c in copies:
        c.wait()
    leaf = jnp.zeros_like(slots)
    for j in range(OFFSETS):
        row = slot_of(jnp.int32(j - 10)) * BLOCK + TABLE_ROW + (j // 16) * 16
        rows = table[pl.ds(pl.multiple_of(row, 16), 16), :].astype(jnp.float32)
        line = jnp.broadcast_to(rows[j % 16 : j % 16 + 1, :], (8, 128)).astype(jnp.int32)
        here = jnp.take_along_axis(line, c_of, axis=1)
        leaf = jnp.where(j_of == j, here, leaf)
    leaf = leaf & (LEAVES - 1)
    found[...] = (row_of + (leaf >> 2) * 32) * 4 + (leaf & 3)
    to_scalars = pltpu.make_async_copy(found, scalars, scalar_sem)
    to_scalars.start()
    to_scalars.wait()

    quarter = lane_index(32) // HALF

    def source(k, t):
        code = scalars[k, t]
        block = table[pl.ds(pl.multiple_of(code >> 2, 32), 32), :].astype(jnp.float32)
        return pltpu.roll(block, (((k & 3) - code) & 3) * HALF, 1)

    def left_side(t):
        parts = []
        for m in range(2):
            part = source(4 * m, t)
            for a in range(1, 4):
                part = jnp.where(quarter == a, source(4 * m + a, t), part)
            parts.append(part.astype(jnp.bfloat16))
        return jnp.concatenate(parts, axis=1)

    def right_side(t):
        return jnp.concatenate(
            [turned[pl.ds(pl.multiple_of(type_ref[k, t] * HALF, HALF), HALF), :] for k in range(FAR)], axis=0
        )

    for j, near_ref in enumerate((near0, near1)):

        @pl.loop(0, LEAVES // 2, step=16)
        def _(i):
            leaves = [j * (LEAVES // 2) + i + u for u in range(16)]
            lefts = [left_side(t) for t in leaves]
            both = [dot(x, right_side(t)) for x, t in zip(lefts, leaves)]
            nodes = [node_ref[pl.ds(pl.multiple_of((t >> 3) * 16, 16), 16), :] for t in leaves[::8]]
            inherited = [dot(nodes[u // 8], down_buf[t]) for u, t in enumerate(leaves)]
            total = [(p[:16] + pltpu.roll(p[16:], RANK, 1))[:, :RANK] + q for p, q in zip(both, inherited)]
            out = [dot(p.astype(jnp.bfloat16), rows_buf[t]) for p, t in zip(total, leaves)]
            near = near_ref[:, pl.ds(pl.multiple_of(i * PANEL, 16 * PANEL), 16 * PANEL)]
            at = pl.multiple_of(leaves[0] * PANEL, 16 * PANEL)
            out_ref[:, pl.ds(at, 16 * PANEL)] = jnp.concatenate(out, axis=1) + near


def far_field(slots, types, pieces, extra, turned, row_basis, down_leaf, near, node_local):
    smem = pl.BlockSpec(memory_space=pltpu.SMEM)
    vmem = pl.BlockSpec(memory_space=pltpu.VMEM)
    hbm = pl.BlockSpec(memory_space=pl.ANY)
    return pl.pallas_call(
        far_kernel,
        in_specs=[vmem, smem] + [hbm] * 7 + [vmem] * 6,
        out_specs=vmem,
        out_shape=jax.ShapeDtypeStruct((16, LEAVES * PANEL), jnp.float32),
        scratch_shapes=[
            pltpu.VMEM((26 * BLOCK, 128), jnp.bfloat16),
            pltpu.VMEM((8, 128), jnp.int32),
            pltpu.SMEM((8, 128), jnp.int32),
            pltpu.SemaphoreType.DMA((7,)),
            pltpu.SemaphoreType.DMA,
        ],
        compiler_params=pltpu.CompilerParams(vmem_limit_bytes=16 << 20),
        cost_estimate=pl.CostEstimate(flops=1000, bytes_accessed=1000, transcendentals=0),
        name="far_field",
    )(slots, types, *pieces, extra, turned, row_basis, down_leaf, *near, node_local)


def per_device(
    loads,
    col_basis,
    row_basis,
    near_blocks,
    near_src,
    up_leaf,
    down_leaf,
    up_node,
    down_node,
    up_group,
    down_group,
    up_top,
    downward_top_transfer,
    coupling,
    send_table,
    distant_leaf_slot_index,
    far_leaf_type,
    far_group_src,
    far_group_type,
    far_top_src,
    far_top_type,
):
    own, to_first, to_second = up_sweep(
        loads, jnp.swapaxes(col_basis, 1, 2), up_leaf, up_node, up_group[0], jnp.swapaxes(send_table, 0, 1)
    )
    along_x = {d: moved(own, flipped(d)) for d in (3, 1, 2)}
    halo0, halo1 = moved(to_first, line_swap(1, 0)), moved(to_second, line_swap(1, 1))
    turned = turned_couplings(jnp.transpose(coupling, (1, 2, 0)).reshape(2, HALF * RANK, TYPES))
    x1, x2, x3, turned, halo0, halo1 = lax.optimization_barrier(
        (along_x[1], along_x[2], along_x[3], turned, halo0, halo1)
    )
    mine, group, tail = joined(own, x1, x2, x3)
    along_z = [moved(group, flipped(8 * d)) for d in (1, 2, 3)]
    *along_z, mine, tail = lax.optimization_barrier((*along_z, mine, tail))
    extra = [moved(tail, two_blocks_away())]
    z0, z1 = moved(mine, line_swap(8, 0)), moved(mine, line_swap(8, 1))
    column = jnp.concatenate([group] + along_z)
    column = jnp.concatenate([column, moved(column, CORE_SWAP)])
    y1 = moved(column, flipped(32))
    column, halo0, halo1 = lax.optimization_barrier((column, halo0, halo1))
    near0 = near_field(near_src.T, halo0, loads, halo1, near_blocks, 0, LEAVES // 2)
    y1, near0, halo0 = lax.optimization_barrier((y1, near0, halo0))
    column = jnp.concatenate([column, y1])
    y2 = moved(column, flipped(64))
    near1 = near_field(near_src.T, halo0, loads, halo1, near_blocks, LEAVES // 2, LEAVES // 2)
    y2, near1, z0, z1, *extra = lax.optimization_barrier((y2, near1, z0, z1, *extra))
    theirs = moved(mine, CORE_SWAP)
    swapped = [moved(z0, CORE_SWAP), moved(z1, CORE_SWAP)]
    (extra,) = extra
    node_local = down_sweep(
        far_group_src,
        far_group_type,
        far_top_src,
        far_top_type,
        [column, y2],
        up_top.reshape(8, 4 * RANK, RANK),
        downward_top_transfer,
        turned,
        down_group[0],
        down_node,
    )
    pieces = [mine, theirs, z0, swapped[0], z1, swapped[1]]
    return far_field(
        distant_leaf_slot_index.T,
        far_leaf_type.T,
        pieces,
        extra,
        turned,
        jnp.swapaxes(row_basis, 1, 2),
        down_leaf,
        [near0, near1],
        node_local,
    )


def solution(mesh):
    whole, split = P(), P(AXES)
    return jax.shard_map(
        per_device,
        mesh=mesh,
        in_specs=(
            P(None, AXES),
            split, split, split, split, split, split, split, split, split, split,
            whole, whole, whole,
            split, split, split,
            P("leaf"), P("leaf"),
            whole, whole,
        ),
        out_specs=P(None, AXES),
        check_vma=False,
    )
```

```python
import functools

import jax
import jax.numpy as jnp
from jax import lax
from jax.experimental import pallas as pl
from jax.experimental.pallas import tpu as pltpu
from jax.sharding import PartitionSpec as P

AXES = ("leaf", "sub")
DEVICES = 128
RANK = 64
PANEL = 128
LEAVES = 64
FAR = 8
NEAR = 6
HALO = 32
OFFSETS = 21
SLOTS = 48
TYPES = 316
HALF = 32
TYPE_ROWS = 328
VMEM = 60 << 20
UP_CHUNKS = 2
TERM_ROW = 512
TABLE_ROW = 528
BLOCK = 560
NT = (((1,), (1,)), ((), ()))


def dot(a, b):
    return jnp.dot(a, b, preferred_element_type=jnp.float32)


def dot_nt(a, b):
    return lax.dot_general(a, b, NT, preferred_element_type=jnp.float32)


def lane_index(rows):
    return lax.broadcasted_iota(jnp.int32, (rows, 128), 1)


def place():
    group, sub = lax.axis_index("leaf"), lax.axis_index("sub")
    return group, sub


def moved(value, pairs):
    return lax.ppermute(value, AXES, pairs)


def flipped(bits):
    return [(p, p ^ bits) for p in range(DEVICES)]


def line_swap(step, odd):
    low = [p for p in range(DEVICES - step) if (p // step) % 2 == odd]
    return [(p, p + step) for p in low] + [(p + step, p) for p in low]


CORE_SWAP = flipped(4)


def two_blocks_away():
    pairs = []
    for p in range(DEVICES):
        x, core = p & 3, (p >> 2) & 1
        target = p + 12 if core == 1 else p - 12
        if (x < 2) == (core == 0) and 0 <= target < DEVICES:
            pairs.append((p, target))
    return pairs


def up_kernel(
    x_hbm, cb_hbm, ul_hbm, un_hbm, ug_hbm, table_ref, out_ref, halo0, halo1,
    x_ref, cb_ref, ul_ref, un_ref, ug_ref, lines, sems,
):
    quarter = lane_index(16) // HALF
    per = LEAVES // UP_CHUNKS
    first = [pltpu.make_async_copy(x_hbm, x_ref, sems.at[0])]
    chunks = []
    for j in range(UP_CHUNKS):
        part = pl.ds(j * per, per)
        chunks.append(
            [
                pltpu.make_async_copy(cb_hbm.at[part], cb_ref.at[part], sems.at[3 + j]),
                pltpu.make_async_copy(ul_hbm.at[part], ul_ref.at[part], sems.at[3 + UP_CHUNKS + j]),
            ]
        )
    last = [pltpu.make_async_copy(un_hbm, un_ref, sems.at[1]), pltpu.make_async_copy(ug_hbm, ug_ref, sems.at[2])]
    for c in first + [c for chunk in chunks for c in chunk] + last:
        c.start()
    lines[...] = jnp.zeros_like(lines)
    for j in range(OFFSETS):
        lines[j : j + 1, :SLOTS] = table_ref[j].astype(jnp.float32)
    out_ref[TABLE_ROW:BLOCK, :] = lines[...].astype(jnp.bfloat16)
    first[0].wait()
    lower, upper = x_ref[:, : HALO * PANEL], x_ref[:, HALO * PANEL :]
    odd = jnp.full(lower.shape, place()[1] & 1, jnp.int32) == 1
    halo0[...] = jnp.where(odd, lower, upper)
    halo1[...] = jnp.where(odd, upper, lower)
    nodes = []
    for j in range(UP_CHUNKS):
        for c in chunks[j]:
            c.wait()
        for n in range(j * per // 8, (j + 1) * per // 8):
            node = jnp.zeros((16, RANK), jnp.float32)
            for b in range(2):
                four = range(n * 8 + b * 4, n * 8 + b * 4 + 4)
                x = jnp.concatenate([x_ref[:, t * PANEL : (t + 1) * PANEL] for t in four], axis=0)
                halves = []
                for q in range(2):
                    rows = slice(q * HALF, (q + 1) * HALF)
                    got = dot_nt(x, jnp.concatenate([cb_ref[t, rows, :] for t in four], axis=0))
                    block = got[:16]
                    for a in range(1, 4):
                        block = jnp.where(quarter == a, got[a * 16 : (a + 1) * 16], block)
                    block = block.astype(jnp.bfloat16)
                    halves.append(block)
                    node = node + dot(block, jnp.concatenate([ul_ref[t, rows, :] for t in four], axis=0))
                row = (n * 2 + b) * 32
                out_ref[row : row + 32, :] = jnp.concatenate(halves, axis=0)
            nodes.append(node.astype(jnp.bfloat16))
    for c in last:
        c.wait()
    mid = dot(nodes[0], un_ref[0])
    for n in range(1, len(nodes)):
        mid = mid + dot(nodes[n], un_ref[n])
    term = dot(mid.astype(jnp.bfloat16), ug_ref[...])
    high = term.astype(jnp.bfloat16).astype(jnp.float32)
    parts = jnp.concatenate([high, term - high], axis=1)
    out_ref[TERM_ROW : TERM_ROW + 16, :] = parts.astype(jnp.bfloat16)


def up_sweep(loads, col_basis, up_leaf, up_node, up_group, table):
    vmem = pl.BlockSpec(memory_space=pltpu.VMEM)
    hbm = pl.BlockSpec(memory_space=pl.ANY)
    return pl.pallas_call(
        up_kernel,
        in_specs=[hbm] * 5 + [vmem],
        out_specs=[vmem] * 3,
        out_shape=[jax.ShapeDtypeStruct((BLOCK, 128), jnp.bfloat16)]
        + [jax.ShapeDtypeStruct((16, HALO * PANEL), jnp.bfloat16)] * 2,
        scratch_shapes=[
            pltpu.VMEM((16, LEAVES * PANEL), jnp.bfloat16),
            pltpu.VMEM((LEAVES, RANK, PANEL), jnp.bfloat16),
            pltpu.VMEM((LEAVES, RANK, RANK), jnp.bfloat16),
            pltpu.VMEM((8, RANK, RANK), jnp.bfloat16),
            pltpu.VMEM((RANK, RANK), jnp.bfloat16),
            pltpu.VMEM((32, 128), jnp.float32),
            pltpu.SemaphoreType.DMA((3 + 2 * UP_CHUNKS,)),
        ],
        compiler_params=pltpu.CompilerParams(vmem_limit_bytes=VMEM),
        cost_estimate=pl.CostEstimate(flops=1000, bytes_accessed=1000, transcendentals=0),
        name="up_sweep",
    )(loads, col_basis, up_leaf, up_node, up_group, table)


def turn_kernel(k_ref, out_ref, table):
    step = pl.program_id(0)
    per_step = k_ref.shape[1] // RANK
    for r in range(per_step):
        rows = slice(r * RANK, (r + 1) * RANK)
        both = jnp.concatenate([k_ref[0, rows, :], k_ref[1, rows, :]], axis=0).astype(jnp.float32)
        row = pl.multiple_of((step * per_step + r) * TYPE_ROWS, 8)
        table[pl.ds(row, TYPES), :] = both.T

    @pl.when(step == pl.num_programs(0) - 1)
    def _():
        @pl.loop(0, TYPES // 4)
        def _(i):
            for u in range(4):
                t = i * 4 + u
                matrix = table[pl.ds(t, HALF, stride=TYPE_ROWS), :].astype(jnp.bfloat16)
                out_ref[pl.ds(pl.multiple_of(t * HALF, HALF), HALF), :] = matrix


def turned_couplings(coupling):
    steps = 4
    rows = TYPES * HALF
    return pl.pallas_call(
        turn_kernel,
        grid=(steps,),
        in_specs=[pl.BlockSpec((2, HALF * RANK // steps, TYPES), lambda i: (0, i, 0))],
        out_specs=pl.BlockSpec((rows, 128), lambda i: (0, 0)),
        out_shape=jax.ShapeDtypeStruct((rows, 128), jnp.bfloat16),
        scratch_shapes=[pltpu.VMEM((HALF * TYPE_ROWS, 128), jnp.float32)],
        compiler_params=pltpu.CompilerParams(vmem_limit_bytes=16 << 20),
        cost_estimate=pl.CostEstimate(flops=1000, bytes_accessed=1000, transcendentals=0),
        name="turn_couplings",
    )(coupling)


def near_kernel(first, src, halo0, own_ref, halo1, blocks_hbm, out_ref, all_x, blocks, sems):
    chunks = sems.shape[0]
    count = blocks.shape[0]
    per = count // chunks

    def copy(j):
        return pltpu.make_async_copy(
            blocks_hbm.at[pl.ds(first + j * per, per)], blocks.at[pl.ds(j * per, per)], sems.at[j]
        )

    for j in range(chunks):
        copy(j).start()
    group, sub = place()
    one, two = halo0[...], halo1[...]
    odd = jnp.full(one.shape, sub & 1, jnp.int32) == 1
    all_x[:, : HALO * PANEL] = jnp.where(odd, one, two)
    all_x[:, HALO * PANEL : (HALO + LEAVES) * PANEL] = own_ref[...]
    all_x[:, (HALO + LEAVES) * PANEL :] = jnp.where(odd, two, one)
    start = (group * 4 + sub) * LEAVES - HALO

    @pl.loop(0, chunks)
    def _(j):
        copy(j).wait()
        out = []
        for u in range(per):
            t = j * per + u
            x = []
            for k in range(NEAR):
                i = src[k, first + t] - start
                x.append(all_x[:, pl.ds(pl.multiple_of(i * PANEL, PANEL), PANEL)])
            row = jnp.concatenate([blocks[t, k] for k in range(NEAR)], axis=1)
            out.append(dot_nt(jnp.concatenate(x, axis=1), row))
        at = pl.multiple_of(j * (per * PANEL), per * PANEL)
        out_ref[:, pl.ds(at, per * PANEL)] = jnp.concatenate(out, axis=1)


def near_field(src, halo0, own, halo1, blocks, first, count):
    chunks = 4
    vmem = pl.BlockSpec(memory_space=pltpu.VMEM)
    return pl.pallas_call(
        functools.partial(near_kernel, first),
        in_specs=[pl.BlockSpec(memory_space=pltpu.SMEM), vmem, vmem, vmem, pl.BlockSpec(memory_space=pl.ANY)],
        out_specs=vmem,
        out_shape=jax.ShapeDtypeStruct((16, count * PANEL), jnp.float32),
        scratch_shapes=[
            pltpu.VMEM((16, (2 * HALO + LEAVES) * PANEL), jnp.bfloat16),
            pltpu.VMEM((count, NEAR, PANEL, PANEL), jnp.bfloat16),
            pltpu.SemaphoreType.DMA((chunks,)),
        ],
        compiler_params=pltpu.CompilerParams(vmem_limit_bytes=52 << 20),
        cost_estimate=pl.CostEstimate(flops=1000, bytes_accessed=1000, transcendentals=0),
        name="near_field",
    )(src, halo0, own, halo1, blocks)


def join_kernel(own, x1, x2, x3, mine_ref, group_ref):
    total = jnp.zeros((16, 128), jnp.float32)
    for d, ref in enumerate((own, x1, x2, x3)):
        mine_ref[d * BLOCK : (d + 1) * BLOCK, :] = ref[...]
        total = total + ref[TERM_ROW : TERM_ROW + 16, :].astype(jnp.float32)
    group_ref[...] = (total + pltpu.roll(total, RANK, 1)).astype(jnp.bfloat16)


def joined(*blocks):
    vmem = pl.BlockSpec(memory_space=pltpu.VMEM)
    return pl.pallas_call(
        join_kernel,
        in_specs=[vmem] * 4,
        out_specs=[vmem] * 2,
        out_shape=[
            jax.ShapeDtypeStruct((4 * BLOCK, 128), jnp.bfloat16),
            jax.ShapeDtypeStruct((16, 128), jnp.bfloat16),
        ],
        compiler_params=pltpu.CompilerParams(vmem_limit_bytes=8 << 20),
        cost_estimate=pl.CostEstimate(flops=1000, bytes_accessed=1000, transcendentals=0),
        name="join_blocks",
    )(*blocks)


def down_kernel(
    far_src, far_type, top_src, top_type, c0, c1, ut_ref, dt_ref, turned_ref, dg_ref, dn_ref, out_ref,
    groups, tops, couplings, own_dt, sems,
):
    group, _ = place()
    y, z, parent = group >> 3, (group >> 1) & 3, group >> 2
    left = lax.broadcasted_iota(jnp.int32, (64, 128), 1) < RANK
    first_core = jnp.full((64, 128), group & 1, jnp.int32) == 0
    for j in range(4):
        ref = (c0, c1)[j // 2]
        at = (j % 2) * 128
        own, other = ref[at : at + 64, :], ref[at + 64 : at + 128, :]
        groups[j * 64 : (j + 1) * 64, :] = jnp.where(left == first_core, own, other)

    def block(yy, zz):
        at = (y ^ yy) * 4 + (z ^ zz)
        return groups[pl.ds(pl.multiple_of(at * 16, 16), 16), :]

    kinds = [far_type[0, k] for k in range(FAR)] + [top_type[parent, k] for k in range(FAR)]
    copies = [
        pltpu.make_async_copy(
            turned_ref.at[pl.ds(pl.multiple_of(kind * HALF, HALF), HALF), :],
            couplings.at[pl.ds(j * HALF, HALF), :],
            sems.at[j],
        )
        for j, kind in enumerate(kinds)
    ]
    copies.append(pltpu.make_async_copy(dt_ref.at[group], own_dt, sems.at[2 * FAR]))
    for c in copies:
        c.start()

    def coupling(j):
        return couplings[j * HALF : (j + 1) * HALF, :]

    def folded(total):
        return (total[:16] + pltpu.roll(total[16:], RANK, 1))[:, :RANK]

    for h in range(8):
        yy, zz = h // 2, 2 * (h % 2)
        four = jnp.concatenate([block(yy, zz), block(yy, zz + 1)], axis=1)
        top = dot(four, ut_ref[h])
        tops[h] = jnp.concatenate([top[:, :HALF], top[:, HALF:]], axis=0).astype(jnp.bfloat16)
    for c in copies:
        c.wait()
    by_group = jnp.zeros((32, 128), jnp.float32)
    by_top = jnp.zeros((32, 128), jnp.float32)
    for k in range(FAR):
        g = far_src[0, k]
        pair = block(g >> 3, (g >> 1) & 3).astype(jnp.float32)
        turn = (g & 1) * RANK
        halves = [pltpu.roll(pair, turn, 1)[:, :HALF], pltpu.roll(pair, turn + 3 * HALF, 1)[:, :HALF]]
        by_group = by_group + dot(jnp.concatenate(halves, axis=0).astype(jnp.bfloat16), coupling(k))
        by_top = by_top + dot(tops[top_src[parent, k]], coupling(FAR + k))
    top_local = folded(by_top).astype(jnp.bfloat16)
    group_local = (folded(by_group) + dot(top_local, own_dt[...])).astype(jnp.bfloat16)
    mid_local = dot(group_local, dg_ref[...]).astype(jnp.bfloat16)
    for n in range(8):
        out_ref[n * 16 : (n + 1) * 16, :] = dot(mid_local, dn_ref[n]).astype(jnp.bfloat16)


def down_sweep(far_src, far_type, top_src, top_type, groups, up_top, down_top, turned, down_group, down_node):
    smem = pl.BlockSpec(memory_space=pltpu.SMEM)
    vmem = pl.BlockSpec(memory_space=pltpu.VMEM)
    hbm = pl.BlockSpec(memory_space=pl.ANY)
    return pl.pallas_call(
        down_kernel,
        in_specs=[smem] * 4 + [vmem] * 3 + [hbm] * 2 + [vmem] * 2,
        out_specs=vmem,
        out_shape=jax.ShapeDtypeStruct((128, RANK), jnp.bfloat16),
        scratch_shapes=[
            pltpu.VMEM((256, 128), jnp.bfloat16),
            pltpu.VMEM((8, 32, HALF), jnp.bfloat16),
            pltpu.VMEM((2 * FAR * HALF, 128), jnp.bfloat16),
            pltpu.VMEM((RANK, RANK), jnp.bfloat16),
            pltpu.SemaphoreType.DMA((2 * FAR + 1,)),
        ],
        compiler_params=pltpu.CompilerParams(vmem_limit_bytes=8 << 20),
        cost_estimate=pl.CostEstimate(flops=1000, bytes_accessed=1000, transcendentals=0),
        name="down_sweep",
    )(far_src, far_type, top_src, top_type, *groups, up_top, down_top, turned, down_group, down_node)


def far_kernel(
    slot_ref, type_ref, g0, g1, z0, z1, z2, z3, e0, e1, turned, rows_buf, down_buf, near0, near1, node_ref,
    out_ref, table, found, scalars, sems, scalar_sem,
):
    copies = []
    for j, ref in enumerate((g0, g1, z0, z1, z2, z3)):
        copies.append((ref, table.at[pl.ds(j * 4 * BLOCK, 4 * BLOCK), :]))
    for j, ref in enumerate((e0, e1)):
        copies.append((ref, table.at[pl.ds((24 + j) * BLOCK, BLOCK), :]))
    copies = [pltpu.make_async_copy(source, target, sems.at[j]) for j, (source, target) in enumerate(copies)]
    for c in copies:
        c.start()

    group, x = place()
    core, block = group & 1, group >> 1
    i_in_block = core * 4 + x

    def slot_of(offset):
        at = i_in_block + offset
        away = at >> 3
        d = (x ^ at) & 3
        same = jnp.where(((at >> 2) & 1) == core, 0, 4)
        first = jnp.where((block & 1) == 0, 1, -1)
        base = jnp.where(away == 0, 0, jnp.where(away == first, 8, 16))
        inside = base + same + d
        return jnp.where((away > 1) | (away < -1), 22 + d, inside)

    found[...] = jnp.zeros_like(found)
    found[:, :LEAVES] = slot_ref[...]
    slots = found[...]
    j_of = (slots * 1366) >> 16
    c_of = slots - j_of * SLOTS
    row_of = slot_of(j_of - 10) * BLOCK
    for c in copies:
        c.wait()
    leaf = jnp.zeros_like(slots)
    for j in range(OFFSETS):
        row = slot_of(jnp.int32(j - 10)) * BLOCK + TABLE_ROW + (j // 16) * 16
        rows = table[pl.ds(pl.multiple_of(row, 16), 16), :].astype(jnp.float32)
        line = jnp.broadcast_to(rows[j % 16 : j % 16 + 1, :], (8, 128)).astype(jnp.int32)
        here = jnp.take_along_axis(line, c_of, axis=1)
        leaf = jnp.where(j_of == j, here, leaf)
    leaf = leaf & (LEAVES - 1)
    found[...] = (row_of + (leaf >> 2) * 32) * 4 + (leaf & 3)
    to_scalars = pltpu.make_async_copy(found, scalars, scalar_sem)
    to_scalars.start()
    to_scalars.wait()

    quarter = lane_index(32) // HALF

    def source(k, t):
        code = scalars[k, t]
        block = table[pl.ds(pl.multiple_of(code >> 2, 32), 32), :].astype(jnp.float32)
        return pltpu.roll(block, (((k & 3) - code) & 3) * HALF, 1)

    def left_side(t):
        parts = []
        for m in range(2):
            part = source(4 * m, t)
            for a in range(1, 4):
                part = jnp.where(quarter == a, source(4 * m + a, t), part)
            parts.append(part.astype(jnp.bfloat16))
        return jnp.concatenate(parts, axis=1)

    def right_side(t):
        return jnp.concatenate(
            [turned[pl.ds(pl.multiple_of(type_ref[k, t] * HALF, HALF), HALF), :] for k in range(FAR)], axis=0
        )

    for j, near_ref in enumerate((near0, near1)):

        @pl.loop(0, LEAVES // 2, step=16)
        def _(i):
            leaves = [j * (LEAVES // 2) + i + u for u in range(16)]
            lefts = [left_side(t) for t in leaves]
            both = [dot(x, right_side(t)) for x, t in zip(lefts, leaves)]
            nodes = [node_ref[pl.ds(pl.multiple_of((t >> 3) * 16, 16), 16), :] for t in leaves[::8]]
            inherited = [dot(nodes[u // 8], down_buf[t]) for u, t in enumerate(leaves)]
            total = [(p[:16] + pltpu.roll(p[16:], RANK, 1))[:, :RANK] + q for p, q in zip(both, inherited)]
            out = [dot(p.astype(jnp.bfloat16), rows_buf[t]) for p, t in zip(total, leaves)]
            near = near_ref[:, pl.ds(pl.multiple_of(i * PANEL, 16 * PANEL), 16 * PANEL)]
            at = pl.multiple_of(leaves[0] * PANEL, 16 * PANEL)
            out_ref[:, pl.ds(at, 16 * PANEL)] = jnp.concatenate(out, axis=1) + near


def far_field(slots, types, pieces, extra, turned, row_basis, down_leaf, near, node_local):
    smem = pl.BlockSpec(memory_space=pltpu.SMEM)
    vmem = pl.BlockSpec(memory_space=pltpu.VMEM)
    hbm = pl.BlockSpec(memory_space=pl.ANY)
    return pl.pallas_call(
        far_kernel,
        in_specs=[vmem, smem] + [hbm] * 8 + [vmem] * 6,
        out_specs=vmem,
        out_shape=jax.ShapeDtypeStruct((16, LEAVES * PANEL), jnp.float32),
        scratch_shapes=[
            pltpu.VMEM((26 * BLOCK, 128), jnp.bfloat16),
            pltpu.VMEM((8, 128), jnp.int32),
            pltpu.SMEM((8, 128), jnp.int32),
            pltpu.SemaphoreType.DMA((8,)),
            pltpu.SemaphoreType.DMA,
        ],
        compiler_params=pltpu.CompilerParams(vmem_limit_bytes=16 << 20),
        cost_estimate=pl.CostEstimate(flops=1000, bytes_accessed=1000, transcendentals=0),
        name="far_field",
    )(slots, types, *pieces, *extra, turned, row_basis, down_leaf, *near, node_local)


def per_device(
    loads,
    col_basis,
    row_basis,
    near_blocks,
    near_src,
    up_leaf,
    down_leaf,
    up_node,
    down_node,
    up_group,
    down_group,
    up_top,
    downward_top_transfer,
    coupling,
    send_table,
    distant_leaf_slot_index,
    far_leaf_type,
    far_group_src,
    far_group_type,
    far_top_src,
    far_top_type,
):
    own, to_first, to_second = up_sweep(
        loads, jnp.swapaxes(col_basis, 1, 2), up_leaf, up_node, up_group[0], jnp.swapaxes(send_table, 0, 1)
    )
    along_x = {d: moved(own, flipped(d)) for d in (3, 1, 2)}
    halo0, halo1 = moved(to_first, line_swap(1, 0)), moved(to_second, line_swap(1, 1))
    x1, x2, x3, coupling = lax.optimization_barrier((along_x[1], along_x[2], along_x[3], coupling))
    tail = moved(own, two_blocks_away())
    mine, group = joined(own, x1, x2, x3)
    along_z = [moved(group, flipped(8 * d)) for d in (1, 2, 3)]
    *along_z, mine, tail, halo0, halo1 = lax.optimization_barrier((*along_z, mine, tail, halo0, halo1))
    z0, z1 = moved(mine, line_swap(8, 0)), moved(mine, line_swap(8, 1))
    column = jnp.concatenate([group] + along_z)
    column = jnp.concatenate([column, moved(column, CORE_SWAP)])
    y1 = moved(column, flipped(32))
    column, halo0, halo1, tail = lax.optimization_barrier((column, halo0, halo1, tail))
    extra = [moved(tail, flipped(2)), moved(tail, flipped(3))]
    near0 = near_field(near_src.T, halo0, loads, halo1, near_blocks, 0, LEAVES // 2)
    near1 = near_field(near_src.T, halo0, loads, halo1, near_blocks, LEAVES // 2, LEAVES // 2)
    y1, near0, near1, coupling = lax.optimization_barrier((y1, near0, near1, coupling))
    turned = turned_couplings(jnp.transpose(coupling, (1, 2, 0)).reshape(2, HALF * RANK, TYPES))
    column = jnp.concatenate([column, y1])
    y2 = moved(column, flipped(64))
    y2, turned, mine, z0, z1, *extra = lax.optimization_barrier((y2, turned, mine, z0, z1, *extra))
    theirs = moved(mine, CORE_SWAP)
    swapped = [moved(z0, CORE_SWAP), moved(z1, CORE_SWAP)]
    node_local = down_sweep(
        far_group_src,
        far_group_type,
        far_top_src,
        far_top_type,
        [column, y2],
        up_top.reshape(8, 4 * RANK, RANK),
        downward_top_transfer,
        turned,
        down_group[0],
        down_node,
    )
    pieces = [mine, theirs, z0, swapped[0], z1, swapped[1]]
    return far_field(
        distant_leaf_slot_index.T,
        far_leaf_type.T,
        pieces,
        extra,
        turned,
        jnp.swapaxes(row_basis, 1, 2),
        down_leaf,
        [near0, near1],
        node_local,
    )


def solution(mesh):
    whole, split = P(), P(AXES)
    return jax.shard_map(
        per_device,
        mesh=mesh,
        in_specs=(
            P(None, AXES),
            split, split, split, split, split, split, split, split, split, split,
            whole, whole, whole,
            split, split, split,
            P("leaf"), P("leaf"),
            whole, whole,
        ),
        out_specs=P(None, AXES),
        check_vma=False,
    )
```

```python
import functools

import jax
import jax.numpy as jnp
from jax import lax
from jax.experimental import pallas as pl
from jax.experimental.pallas import tpu as pltpu
from jax.sharding import PartitionSpec as P

AXES = ("leaf", "sub")
DEVICES = 128
RANK = 64
PANEL = 128
LEAVES = 64
FAR = 8
NEAR = 6
HALO = 32
OFFSETS = 21
SLOTS = 48
TYPES = 316
HALF = 32
TYPE_ROWS = 328
VMEM = 60 << 20
UP_CHUNKS = 2
TERM_ROW = 512
TABLE_ROW = 528
BLOCK = 560
NT = (((1,), (1,)), ((), ()))


def dot(a, b):
    return jnp.dot(a, b, preferred_element_type=jnp.float32)


def dot_nt(a, b):
    return lax.dot_general(a, b, NT, preferred_element_type=jnp.float32)


def lane_index(rows):
    return lax.broadcasted_iota(jnp.int32, (rows, 128), 1)


def place():
    group, sub = lax.axis_index("leaf"), lax.axis_index("sub")
    return group, sub


def moved(value, pairs):
    return lax.ppermute(value, AXES, pairs)


def flipped(bits):
    return [(p, p ^ bits) for p in range(DEVICES)]


def line_swap(step, odd):
    low = [p for p in range(DEVICES - step) if (p // step) % 2 == odd]
    return [(p, p + step) for p in low] + [(p + step, p) for p in low]


CORE_SWAP = flipped(4)


def two_blocks_away():
    pairs = []
    for p in range(DEVICES):
        x, core = p & 3, (p >> 2) & 1
        target = p + 12 if core == 1 else p - 12
        if (x < 2) == (core == 0) and 0 <= target < DEVICES:
            pairs.append((p, target))
    return pairs


def up_kernel(
    x_hbm, cb_hbm, ul_hbm, un_hbm, ug_hbm, table_ref, out_ref, halo0, halo1,
    x_ref, cb_ref, ul_ref, un_ref, ug_ref, lines, sems,
):
    quarter = lane_index(16) // HALF
    per = LEAVES // UP_CHUNKS
    first = [pltpu.make_async_copy(x_hbm, x_ref, sems.at[0])]
    chunks = []
    for j in range(UP_CHUNKS):
        part = pl.ds(j * per, per)
        chunks.append(
            [
                pltpu.make_async_copy(cb_hbm.at[part], cb_ref.at[part], sems.at[3 + j]),
                pltpu.make_async_copy(ul_hbm.at[part], ul_ref.at[part], sems.at[3 + UP_CHUNKS + j]),
            ]
        )
    last = [pltpu.make_async_copy(un_hbm, un_ref, sems.at[1]), pltpu.make_async_copy(ug_hbm, ug_ref, sems.at[2])]
    for c in first + [c for chunk in chunks for c in chunk] + last:
        c.start()
    lines[...] = jnp.zeros_like(lines)
    for j in range(OFFSETS):
        lines[j : j + 1, :SLOTS] = table_ref[j].astype(jnp.float32)
    out_ref[TABLE_ROW:BLOCK, :] = lines[...].astype(jnp.bfloat16)
    first[0].wait()
    lower, upper = x_ref[:, : HALO * PANEL], x_ref[:, HALO * PANEL :]
    odd = jnp.full(lower.shape, place()[1] & 1, jnp.int32) == 1
    halo0[...] = jnp.where(odd, lower, upper)
    halo1[...] = jnp.where(odd, upper, lower)
    nodes = []
    for j in range(UP_CHUNKS):
        for c in chunks[j]:
            c.wait()
        for n in range(j * per // 8, (j + 1) * per // 8):
            node = jnp.zeros((16, RANK), jnp.float32)
            for b in range(2):
                four = range(n * 8 + b * 4, n * 8 + b * 4 + 4)
                x = jnp.concatenate([x_ref[:, t * PANEL : (t + 1) * PANEL] for t in four], axis=0)
                halves = []
                for q in range(2):
                    rows = slice(q * HALF, (q + 1) * HALF)
                    got = dot_nt(x, jnp.concatenate([cb_ref[t, rows, :] for t in four], axis=0))
                    block = got[:16]
                    for a in range(1, 4):
                        block = jnp.where(quarter == a, got[a * 16 : (a + 1) * 16], block)
                    block = block.astype(jnp.bfloat16)
                    halves.append(block)
                    node = node + dot(block, jnp.concatenate([ul_ref[t, rows, :] for t in four], axis=0))
                row = (n * 2 + b) * 32
                out_ref[row : row + 32, :] = jnp.concatenate(halves, axis=0)
            nodes.append(node.astype(jnp.bfloat16))
    for c in last:
        c.wait()
    mid = dot(nodes[0], un_ref[0])
    for n in range(1, len(nodes)):
        mid = mid + dot(nodes[n], un_ref[n])
    term = dot(mid.astype(jnp.bfloat16), ug_ref[...])
    high = term.astype(jnp.bfloat16).astype(jnp.float32)
    parts = jnp.concatenate([high, term - high], axis=1)
    out_ref[TERM_ROW : TERM_ROW + 16, :] = parts.astype(jnp.bfloat16)


def up_sweep(loads, col_basis, up_leaf, up_node, up_group, table):
    vmem = pl.BlockSpec(memory_space=pltpu.VMEM)
    hbm = pl.BlockSpec(memory_space=pl.ANY)
    return pl.pallas_call(
        up_kernel,
        in_specs=[hbm] * 5 + [vmem],
        out_specs=[vmem] * 3,
        out_shape=[jax.ShapeDtypeStruct((BLOCK, 128), jnp.bfloat16)]
        + [jax.ShapeDtypeStruct((16, HALO * PANEL), jnp.bfloat16)] * 2,
        scratch_shapes=[
            pltpu.VMEM((16, LEAVES * PANEL), jnp.bfloat16),
            pltpu.VMEM((LEAVES, RANK, PANEL), jnp.bfloat16),
            pltpu.VMEM((LEAVES, RANK, RANK), jnp.bfloat16),
            pltpu.VMEM((8, RANK, RANK), jnp.bfloat16),
            pltpu.VMEM((RANK, RANK), jnp.bfloat16),
            pltpu.VMEM((32, 128), jnp.float32),
            pltpu.SemaphoreType.DMA((3 + 2 * UP_CHUNKS,)),
        ],
        compiler_params=pltpu.CompilerParams(vmem_limit_bytes=VMEM),
        cost_estimate=pl.CostEstimate(flops=1000, bytes_accessed=1000, transcendentals=0),
        name="up_sweep",
    )(loads, col_basis, up_leaf, up_node, up_group, table)


def turn_kernel(k_ref, out_ref, table):
    step = pl.program_id(0)
    per_step = k_ref.shape[1] // RANK
    for r in range(per_step):
        rows = slice(r * RANK, (r + 1) * RANK)
        both = jnp.concatenate([k_ref[0, rows, :], k_ref[1, rows, :]], axis=0).astype(jnp.float32)
        row = pl.multiple_of((step * per_step + r) * TYPE_ROWS, 8)
        table[pl.ds(row, TYPES), :] = both.T

    @pl.when(step == pl.num_programs(0) - 1)
    def _():
        @pl.loop(0, TYPES // 4)
        def _(i):
            for u in range(4):
                t = i * 4 + u
                matrix = table[pl.ds(t, HALF, stride=TYPE_ROWS), :].astype(jnp.bfloat16)
                out_ref[pl.ds(pl.multiple_of(t * HALF, HALF), HALF), :] = matrix


def turned_couplings(coupling):
    steps = 4
    rows = TYPES * HALF
    return pl.pallas_call(
        turn_kernel,
        grid=(steps,),
        in_specs=[pl.BlockSpec((2, HALF * RANK // steps, TYPES), lambda i: (0, i, 0))],
        out_specs=pl.BlockSpec((rows, 128), lambda i: (0, 0)),
        out_shape=jax.ShapeDtypeStruct((rows, 128), jnp.bfloat16),
        scratch_shapes=[pltpu.VMEM((HALF * TYPE_ROWS, 128), jnp.float32)],
        compiler_params=pltpu.CompilerParams(vmem_limit_bytes=16 << 20),
        cost_estimate=pl.CostEstimate(flops=1000, bytes_accessed=1000, transcendentals=0),
        name="turn_couplings",
    )(coupling)


def near_kernel(first, src, halo0, own_ref, halo1, blocks_hbm, out_ref, all_x, blocks, sems):
    chunks = sems.shape[0]
    count = blocks.shape[0]
    per = count // chunks

    def copy(j):
        return pltpu.make_async_copy(
            blocks_hbm.at[pl.ds(first + j * per, per)], blocks.at[pl.ds(j * per, per)], sems.at[j]
        )

    for j in range(chunks):
        copy(j).start()
    group, sub = place()
    one, two = halo0[...], halo1[...]
    odd = jnp.full(one.shape, sub & 1, jnp.int32) == 1
    all_x[:, : HALO * PANEL] = jnp.where(odd, one, two)
    all_x[:, HALO * PANEL : (HALO + LEAVES) * PANEL] = own_ref[...]
    all_x[:, (HALO + LEAVES) * PANEL :] = jnp.where(odd, two, one)
    start = (group * 4 + sub) * LEAVES - HALO

    @pl.loop(0, chunks)
    def _(j):
        copy(j).wait()
        out = []
        for u in range(per):
            t = j * per + u
            x = []
            for k in range(NEAR):
                i = src[k, first + t] - start
                x.append(all_x[:, pl.ds(pl.multiple_of(i * PANEL, PANEL), PANEL)])
            row = jnp.concatenate([blocks[t, k] for k in range(NEAR)], axis=1)
            out.append(dot_nt(jnp.concatenate(x, axis=1), row))
        at = pl.multiple_of(j * (per * PANEL), per * PANEL)
        out_ref[:, pl.ds(at, per * PANEL)] = jnp.concatenate(out, axis=1)


def near_field(src, halo0, own, halo1, blocks, first, count):
    chunks = 4
    vmem = pl.BlockSpec(memory_space=pltpu.VMEM)
    return pl.pallas_call(
        functools.partial(near_kernel, first),
        in_specs=[pl.BlockSpec(memory_space=pltpu.SMEM), vmem, vmem, vmem, pl.BlockSpec(memory_space=pl.ANY)],
        out_specs=vmem,
        out_shape=jax.ShapeDtypeStruct((16, count * PANEL), jnp.float32),
        scratch_shapes=[
            pltpu.VMEM((16, (2 * HALO + LEAVES) * PANEL), jnp.bfloat16),
            pltpu.VMEM((count, NEAR, PANEL, PANEL), jnp.bfloat16),
            pltpu.SemaphoreType.DMA((chunks,)),
        ],
        compiler_params=pltpu.CompilerParams(vmem_limit_bytes=52 << 20),
        cost_estimate=pl.CostEstimate(flops=1000, bytes_accessed=1000, transcendentals=0),
        name="near_field",
    )(src, halo0, own, halo1, blocks)


def join_kernel(own, x1, x2, x3, mine_ref, group_ref):
    total = jnp.zeros((16, 128), jnp.float32)
    for d, ref in enumerate((own, x1, x2, x3)):
        mine_ref[d * BLOCK : (d + 1) * BLOCK, :] = ref[...]
        total = total + ref[TERM_ROW : TERM_ROW + 16, :].astype(jnp.float32)
    group_ref[...] = (total + pltpu.roll(total, RANK, 1)).astype(jnp.bfloat16)


def joined(*blocks):
    vmem = pl.BlockSpec(memory_space=pltpu.VMEM)
    return pl.pallas_call(
        join_kernel,
        in_specs=[vmem] * 4,
        out_specs=[vmem] * 2,
        out_shape=[
            jax.ShapeDtypeStruct((4 * BLOCK, 128), jnp.bfloat16),
            jax.ShapeDtypeStruct((16, 128), jnp.bfloat16),
        ],
        compiler_params=pltpu.CompilerParams(vmem_limit_bytes=8 << 20),
        cost_estimate=pl.CostEstimate(flops=1000, bytes_accessed=1000, transcendentals=0),
        name="join_blocks",
    )(*blocks)


def down_kernel(
    far_src, far_type, top_src, top_type, c0, c1, ut_ref, dt_ref, turned_ref, dg_ref, dn_ref, out_ref,
    groups, tops, couplings, own_dt, sems,
):
    group, _ = place()
    y, z, parent = group >> 3, (group >> 1) & 3, group >> 2
    left = lax.broadcasted_iota(jnp.int32, (64, 128), 1) < RANK
    first_core = jnp.full((64, 128), group & 1, jnp.int32) == 0
    for j in range(4):
        ref = (c0, c1)[j // 2]
        at = (j % 2) * 128
        own, other = ref[at : at + 64, :], ref[at + 64 : at + 128, :]
        groups[j * 64 : (j + 1) * 64, :] = jnp.where(left == first_core, own, other)

    def block(yy, zz):
        at = (y ^ yy) * 4 + (z ^ zz)
        return groups[pl.ds(pl.multiple_of(at * 16, 16), 16), :]

    kinds = [far_type[0, k] for k in range(FAR)] + [top_type[parent, k] for k in range(FAR)]
    copies = [
        pltpu.make_async_copy(
            turned_ref.at[pl.ds(pl.multiple_of(kind * HALF, HALF), HALF), :],
            couplings.at[pl.ds(j * HALF, HALF), :],
            sems.at[j],
        )
        for j, kind in enumerate(kinds)
    ]
    copies.append(pltpu.make_async_copy(dt_ref.at[group], own_dt, sems.at[2 * FAR]))
    for c in copies:
        c.start()

    def coupling(j):
        return couplings[j * HALF : (j + 1) * HALF, :]

    def folded(total):
        return (total[:16] + pltpu.roll(total[16:], RANK, 1))[:, :RANK]

    for h in range(8):
        yy, zz = h // 2, 2 * (h % 2)
        four = jnp.concatenate([block(yy, zz), block(yy, zz + 1)], axis=1)
        top = dot(four, ut_ref[h])
        tops[h] = jnp.concatenate([top[:, :HALF], top[:, HALF:]], axis=0).astype(jnp.bfloat16)
    for c in copies:
        c.wait()
    by_group = jnp.zeros((32, 128), jnp.float32)
    by_top = jnp.zeros((32, 128), jnp.float32)
    for k in range(FAR):
        g = far_src[0, k]
        pair = block(g >> 3, (g >> 1) & 3).astype(jnp.float32)
        turn = (g & 1) * RANK
        halves = [pltpu.roll(pair, turn, 1)[:, :HALF], pltpu.roll(pair, turn + 3 * HALF, 1)[:, :HALF]]
        by_group = by_group + dot(jnp.concatenate(halves, axis=0).astype(jnp.bfloat16), coupling(k))
        by_top = by_top + dot(tops[top_src[parent, k]], coupling(FAR + k))
    top_local = folded(by_top).astype(jnp.bfloat16)
    group_local = (folded(by_group) + dot(top_local, own_dt[...])).astype(jnp.bfloat16)
    mid_local = dot(group_local, dg_ref[...]).astype(jnp.bfloat16)
    for n in range(8):
        out_ref[n * 16 : (n + 1) * 16, :] = dot(mid_local, dn_ref[n]).astype(jnp.bfloat16)


def down_sweep(far_src, far_type, top_src, top_type, groups, up_top, down_top, turned, down_group, down_node):
    smem = pl.BlockSpec(memory_space=pltpu.SMEM)
    vmem = pl.BlockSpec(memory_space=pltpu.VMEM)
    hbm = pl.BlockSpec(memory_space=pl.ANY)
    return pl.pallas_call(
        down_kernel,
        in_specs=[smem] * 4 + [vmem] * 3 + [hbm] * 2 + [vmem] * 2,
        out_specs=vmem,
        out_shape=jax.ShapeDtypeStruct((128, RANK), jnp.bfloat16),
        scratch_shapes=[
            pltpu.VMEM((256, 128), jnp.bfloat16),
            pltpu.VMEM((8, 32, HALF), jnp.bfloat16),
            pltpu.VMEM((2 * FAR * HALF, 128), jnp.bfloat16),
            pltpu.VMEM((RANK, RANK), jnp.bfloat16),
            pltpu.SemaphoreType.DMA((2 * FAR + 1,)),
        ],
        compiler_params=pltpu.CompilerParams(vmem_limit_bytes=8 << 20),
        cost_estimate=pl.CostEstimate(flops=1000, bytes_accessed=1000, transcendentals=0),
        name="down_sweep",
    )(far_src, far_type, top_src, top_type, *groups, up_top, down_top, turned, down_group, down_node)


def far_kernel(
    slot_ref, type_ref, g0, g1, z0, z1, z2, z3, e0, e1, turned, rows_buf, down_buf, near0, near1, node_ref,
    out_ref, table, found, scalars, sems, scalar_sem,
):
    copies = []
    for j, ref in enumerate((g0, g1, z0, z1, z2, z3)):
        copies.append((ref, table.at[pl.ds(j * 4 * BLOCK, 4 * BLOCK), :]))
    for j, ref in enumerate((e0, e1)):
        copies.append((ref, table.at[pl.ds((24 + j) * BLOCK, BLOCK), :]))
    copies = [pltpu.make_async_copy(source, target, sems.at[j]) for j, (source, target) in enumerate(copies)]
    for c in copies:
        c.start()

    group, x = place()
    core, block = group & 1, group >> 1
    i_in_block = core * 4 + x

    def slot_of(offset):
        at = i_in_block + offset
        away = at >> 3
        d = (x ^ at) & 3
        same = jnp.where(((at >> 2) & 1) == core, 0, 4)
        first = jnp.where((block & 1) == 0, 1, -1)
        base = jnp.where(away == 0, 0, jnp.where(away == first, 8, 16))
        inside = base + same + d
        return jnp.where((away > 1) | (away < -1), 22 + d, inside)

    found[...] = jnp.zeros_like(found)
    found[:, :LEAVES] = slot_ref[...]
    slots = found[...]
    j_of = (slots * 1366) >> 16
    c_of = slots - j_of * SLOTS
    row_of = slot_of(j_of - 10) * BLOCK
    for c in copies:
        c.wait()
    leaf = jnp.zeros_like(slots)
    for j in range(OFFSETS):
        row = slot_of(jnp.int32(j - 10)) * BLOCK + TABLE_ROW + (j // 16) * 16
        rows = table[pl.ds(pl.multiple_of(row, 16), 16), :].astype(jnp.float32)
        line = jnp.broadcast_to(rows[j % 16 : j % 16 + 1, :], (8, 128)).astype(jnp.int32)
        here = jnp.take_along_axis(line, c_of, axis=1)
        leaf = jnp.where(j_of == j, here, leaf)
    leaf = leaf & (LEAVES - 1)
    found[...] = (row_of + (leaf >> 2) * 32) * 4 + (leaf & 3)
    to_scalars = pltpu.make_async_copy(found, scalars, scalar_sem)
    to_scalars.start()
    to_scalars.wait()

    quarter = lane_index(32) // HALF

    def source(k, t):
        code = scalars[k, t]
        block = table[pl.ds(pl.multiple_of(code >> 2, 32), 32), :].astype(jnp.float32)
        return pltpu.roll(block, (((k & 3) - code) & 3) * HALF, 1)

    def left_side(t):
        parts = []
        for m in range(2):
            part = source(4 * m, t)
            for a in range(1, 4):
                part = jnp.where(quarter == a, source(4 * m + a, t), part)
            parts.append(part.astype(jnp.bfloat16))
        return jnp.concatenate(parts, axis=1)

    def right_side(t):
        return jnp.concatenate(
            [turned[pl.ds(pl.multiple_of(type_ref[k, t] * HALF, HALF), HALF), :] for k in range(FAR)], axis=0
        )

    for j, near_ref in enumerate((near0, near1)):

        @pl.loop(0, LEAVES // 2, step=32)
        def _(i):
            leaves = [j * (LEAVES // 2) + i + u for u in range(32)]
            lefts = [left_side(t) for t in leaves]
            both = [dot(x, right_side(t)) for x, t in zip(lefts, leaves)]
            nodes = [node_ref[pl.ds(pl.multiple_of((t >> 3) * 16, 16), 16), :] for t in leaves[::8]]
            inherited = [dot(nodes[u // 8], down_buf[t]) for u, t in enumerate(leaves)]
            total = [(p[:16] + pltpu.roll(p[16:], RANK, 1))[:, :RANK] + q for p, q in zip(both, inherited)]
            out = [dot(p.astype(jnp.bfloat16), rows_buf[t]) for p, t in zip(total, leaves)]
            near = near_ref[:, pl.ds(pl.multiple_of(i * PANEL, 32 * PANEL), 32 * PANEL)]
            at = pl.multiple_of(leaves[0] * PANEL, 32 * PANEL)
            out_ref[:, pl.ds(at, 32 * PANEL)] = jnp.concatenate(out, axis=1) + near


def far_field(slots, types, pieces, extra, turned, row_basis, down_leaf, near, node_local):
    smem = pl.BlockSpec(memory_space=pltpu.SMEM)
    vmem = pl.BlockSpec(memory_space=pltpu.VMEM)
    hbm = pl.BlockSpec(memory_space=pl.ANY)
    return pl.pallas_call(
        far_kernel,
        in_specs=[vmem, smem] + [hbm] * 8 + [vmem] * 6,
        out_specs=vmem,
        out_shape=jax.ShapeDtypeStruct((16, LEAVES * PANEL), jnp.float32),
        scratch_shapes=[
            pltpu.VMEM((26 * BLOCK, 128), jnp.bfloat16),
            pltpu.VMEM((8, 128), jnp.int32),
            pltpu.SMEM((8, 128), jnp.int32),
            pltpu.SemaphoreType.DMA((8,)),
            pltpu.SemaphoreType.DMA,
        ],
        compiler_params=pltpu.CompilerParams(vmem_limit_bytes=16 << 20),
        cost_estimate=pl.CostEstimate(flops=1000, bytes_accessed=1000, transcendentals=0),
        name="far_field",
    )(slots, types, *pieces, *extra, turned, row_basis, down_leaf, *near, node_local)


def per_device(
    loads,
    col_basis,
    row_basis,
    near_blocks,
    near_src,
    up_leaf,
    down_leaf,
    up_node,
    down_node,
    up_group,
    down_group,
    up_top,
    downward_top_transfer,
    coupling,
    send_table,
    distant_leaf_slot_index,
    far_leaf_type,
    far_group_src,
    far_group_type,
    far_top_src,
    far_top_type,
):
    own, to_first, to_second = up_sweep(
        loads, jnp.swapaxes(col_basis, 1, 2), up_leaf, up_node, up_group[0], jnp.swapaxes(send_table, 0, 1)
    )
    along_x = {d: moved(own, flipped(d)) for d in (3, 1, 2)}
    halo0, halo1 = moved(to_first, line_swap(1, 0)), moved(to_second, line_swap(1, 1))
    x1, x2, x3, coupling = lax.optimization_barrier((along_x[1], along_x[2], along_x[3], coupling))
    tail = moved(own, two_blocks_away())
    mine, group = joined(own, x1, x2, x3)
    along_z = [moved(group, flipped(8 * d)) for d in (1, 2, 3)]
    *along_z, mine, tail, halo0, halo1 = lax.optimization_barrier((*along_z, mine, tail, halo0, halo1))
    z0, z1 = moved(mine, line_swap(8, 0)), moved(mine, line_swap(8, 1))
    column = jnp.concatenate([group] + along_z)
    column = jnp.concatenate([column, moved(column, CORE_SWAP)])
    y1 = moved(column, flipped(32))
    column, halo0, halo1, tail = lax.optimization_barrier((column, halo0, halo1, tail))
    extra = [moved(tail, flipped(2)), moved(tail, flipped(3))]
    near0 = near_field(near_src.T, halo0, loads, halo1, near_blocks, 0, LEAVES // 2)
    near1 = near_field(near_src.T, halo0, loads, halo1, near_blocks, LEAVES // 2, LEAVES // 2)
    y1, near0, near1, coupling = lax.optimization_barrier((y1, near0, near1, coupling))
    turned = turned_couplings(jnp.transpose(coupling, (1, 2, 0)).reshape(2, HALF * RANK, TYPES))
    column = jnp.concatenate([column, y1])
    y2 = moved(column, flipped(64))
    y2, turned, mine, z0, z1, *extra = lax.optimization_barrier((y2, turned, mine, z0, z1, *extra))
    theirs = moved(mine, CORE_SWAP)
    swapped = [moved(z0, CORE_SWAP), moved(z1, CORE_SWAP)]
    node_local = down_sweep(
        far_group_src,
        far_group_type,
        far_top_src,
        far_top_type,
        [column, y2],
        up_top.reshape(8, 4 * RANK, RANK),
        downward_top_transfer,
        turned,
        down_group[0],
        down_node,
    )
    pieces = [mine, theirs, z0, swapped[0], z1, swapped[1]]
    return far_field(
        distant_leaf_slot_index.T,
        far_leaf_type.T,
        pieces,
        extra,
        turned,
        jnp.swapaxes(row_basis, 1, 2),
        down_leaf,
        [near0, near1],
        node_local,
    )


def solution(mesh):
    whole, split = P(), P(AXES)
    return jax.shard_map(
        per_device,
        mesh=mesh,
        in_specs=(
            P(None, AXES),
            split, split, split, split, split, split, split, split, split, split,
            whole, whole, whole,
            split, split, split,
            P("leaf"), P("leaf"),
            whole, whole,
        ),
        out_specs=P(None, AXES),
        check_vma=False,
    )
```
